32 devices in a mesh: region: 2 (over x), tm: 8 (over z, y), tile: 2 (over core).
Axes of the slice: x: 2, y: 2, z: 4, core: 2. Of those that a mesh axis runs over, the one named last changes fastest.
Arguments:
- coords: float32 [3, 65536], P(None, ('region', 'tm', 'tile')), parts along dimension 1, may hold values from 0 to 16, as said below
- anomalies: float32 [65536, 128], P(('region', 'tm', 'tile')), parts along dimension 0, may hold values from -6 to 6
- noise_var: float32 [65536], P(('region', 'tm', 'tile')), parts along dimension 0, may hold values from 0.3 to 3
Outputs:
- weights: float32 [65536, 128], P(('region', 'tm', 'tile')), parts along dimension 0
- residual: float32 [65536, 128], P(('region', 'tm', 'tile')), parts along dimension 0
The draws below stay inside these ranges and needn't reach their ends.
There are 2 independent parts, one for each index of `region`. The reference program is written for one: setup_inputs(seed, part) draws one part's arguments, and reference() takes and returns one part's arrays. A program takes and returns all parts, laid end to end along the dimension named above; each array names one. Nothing has to cross between parts.
Inputs may be any that keep to these rules, and one draw needn't show every extreme that they name: `coords`: row 0 holds times in units of the kernel's time support, rising along the observations; observations k * 4096 to (k + 1) * 4096 - 1 have times in [k, k + 1). Rows 1 and 2 are positions in units of the spatial support.
All inputs are finite; a program needn't handle non-finite values.
Results may differ from the reference program's by a relative error of at most 0.0003.
Values sent between devices are 32-bit elements; how exact they have to be, the bound alone decides.
No kernel may reach another device: no remote copies, remote signals or barrier semaphores. Data moves between devices by JAX's collectives and lax.ppermute only.
A program may use at most 64 MiB of HBM per device.

```python
import math
import jax
import jax.numpy as jnp
from jax import lax

SLAB = 4096
NRHS = 128
ITERS = 2
POINTS = 32768


def draw_coords(key, part):
    key = jax.random.fold_in(key, 11)
    time_key, place_key = jax.random.split(key)
    jitter = jax.random.uniform(time_key, (POINTS,), jnp.float32)
    times = (jnp.arange(POINTS, dtype=jnp.float32) + jitter) / float(SLAB)
    spread = float(SLAB) ** 0.5 / 4.0
    places = jax.random.uniform(place_key, (2, POINTS), jnp.float32) * spread
    return jnp.concatenate([times[None, :], places], axis=0)


def levels(key, extent, shards, low, largest):
    level = 1.0
    for axis_at, shards_of in shards:
        heights = jax.random.uniform(jax.random.fold_in(jax.random.fold_in(key, 6), axis_at), (shards_of,), jnp.float32, low / len(shards), largest / len(shards))
        level = level * jnp.repeat(jnp.exp(heights), extent[axis_at] // shards_of).reshape((-1,) + (1,) * (len(extent) - 1 - axis_at))
    return level


def scatter_about(key, dims, width, reach, cuts=(), held_as=jnp.bfloat16):
    array = jax.random.normal(key, dims, jnp.float32) * width
    if len(cuts) > 0:
        array = levels(key, dims, cuts, -0.22, 0.18) * array
    return jnp.clip(array, min=-reach, max=reach).astype(held_as)


def setup_inputs(seed: int = 0, part: int = 0) -> dict:
    splits = jax.random.split(jax.random.key(seed), 4)
    part_keys = jax.random.split(jax.random.fold_in(splits[3], part), 4)
    return {
        "coords": draw_coords(jax.random.fold_in(jax.random.fold_in(splits[3], part), 71), part),
        "anomalies": scatter_about(part_keys[1], (POINTS, NRHS), 1.0, 6.0, ((0, 16),), jnp.float32),
        "noise_var": jnp.clip(jnp.exp(math.log(3.0) - 2.3025851 * jax.random.uniform(part_keys[2], (POINTS,), jnp.float32) ** levels(part_keys[2], (POINTS,), ((0, 16),), -0.2, 0.2)), 0.3, 3.0),
    }


def wendland(dist):
    clipped = jnp.maximum(1.0 - dist, 0.0)
    return clipped * clipped * clipped * clipped * (4.0 * dist + 1.0)

def kernel_tile(rows, cols):
    dtime = jnp.abs(rows[0][:, None] - cols[0][None, :])
    dxpos = rows[1][:, None] - cols[1][None, :]
    dypos = rows[2][:, None] - cols[2][None, :]
    return wendland(dtime) * wendland(jnp.sqrt(dxpos * dxpos + dypos * dypos))

def apply_matrix(coords, noise_var, direction):
    slabs = POINTS // SLAB
    padded_coords = jnp.pad(coords, ((0, 0), (SLAB, SLAB)))
    padded_dir = jnp.pad(direction, ((SLAB, SLAB), (0, 0)))

    def one_slab(index):
        start = (index * SLAB).astype(jnp.int32)
        rows = lax.dynamic_slice_in_dim(coords, start, SLAB, 1)
        cols = lax.dynamic_slice_in_dim(padded_coords, start, 3 * SLAB, 1)
        values = lax.dynamic_slice_in_dim(padded_dir, start, 3 * SLAB, 0)
        return jnp.dot(kernel_tile(rows, cols), values, precision=lax.Precision.HIGHEST, preferred_element_type=jnp.float32)
    image = lax.map(one_slab, jnp.arange(slabs, dtype=jnp.int32))
    return image.reshape(POINTS, -1) + noise_var[:, None] * direction

def reference(coords, anomalies, noise_var):
    weights = jnp.zeros_like(anomalies)
    residual = anomalies
    direction = anomalies
    norm_now = lax.optimization_barrier(jnp.sum(residual * residual, axis=0))
    for step in range(ITERS):
        image = apply_matrix(coords, noise_var, direction)
        alpha = norm_now / lax.optimization_barrier(jnp.sum(direction * image, axis=0))
        weights = weights + alpha * direction
        residual = residual - alpha * image
        norm_next = lax.optimization_barrier(jnp.sum(residual * residual, axis=0))
        direction = residual + norm_next / norm_now * direction
        norm_now = norm_next
    return (weights, residual)
```

```python
import functools

import jax
import jax.numpy as jnp
from jax import lax
from jax.experimental import pallas as pl
from jax.experimental.pallas import tpu as pltpu
from jax.sharding import PartitionSpec as P

LANES = 128
WINDOW = 256
ROWS = 192
SLOTS = 56
FAR = 1.0e6
F32 = jnp.float32
BF16 = jnp.bfloat16
MIB = 1 << 20


def vmem_spec():
    return pl.BlockSpec(memory_space=pltpu.VMEM)


def smem_spec():
    return pl.BlockSpec(memory_space=pltpu.SMEM)


def split2(value):
    high = value.astype(BF16)
    low = (value - high.astype(F32)).astype(BF16)
    return high, low


def split3(value):
    high = value.astype(BF16)
    rest = value - high.astype(F32)
    mid = rest.astype(BF16)
    low = (rest - mid.astype(F32)).astype(BF16)
    return high, mid, low


def sort_kernel(points, coords, noise, values, sorted_values, lanes, rows, rank_row, rank_col, xcol, pieces, small):
    groups = points // LANES
    for g in range(groups):
        part = coords[1:2, g * LANES : (g + 1) * LANES]
        xcol[g * LANES : (g + 1) * LANES, :] = jnp.transpose(jnp.broadcast_to(part, (LANES, LANES)))

    xrow = [jnp.broadcast_to(coords[1:2, g * LANES : (g + 1) * LANES], (8, LANES)) for g in range(groups)]
    lane = lax.broadcasted_iota(jnp.int32, (8, LANES), 1)
    sub = lax.broadcasted_iota(jnp.int32, (8, LANES), 0)
    counts = [jnp.zeros((8, LANES), F32) for _ in range(groups)]
    for jg in range(groups):

        def count(step, carry):
            at = pl.multiple_of(jg * LANES + step * 8, 8)
            mine = xcol[pl.ds(at, 8), :]
            out = []
            for ig in range(groups):
                if ig == jg:
                    before = jnp.logical_or(
                        mine < xrow[ig],
                        jnp.logical_and(mine == xrow[ig], sub + step * 8 < lane),
                    )
                elif ig > jg:
                    before = mine <= xrow[ig]
                else:
                    before = mine < xrow[ig]
                out.append(carry[ig] + jnp.where(before, 1.0, 0.0))
            return tuple(out)

        counts = lax.fori_loop(0, LANES // 8, count, tuple(counts))
    for g in range(groups):
        total = jnp.sum(counts[g], axis=0, keepdims=True)
        rank_row[0:1, g * LANES : (g + 1) * LANES] = total
        rank_col[g * LANES : (g + 1) * LANES, :] = jnp.transpose(jnp.broadcast_to(total, (LANES, LANES)))

    high, low = split2(values[...])
    pieces[:, 0:LANES] = high
    pieces[:, LANES : 2 * LANES] = low
    stacked = jnp.concatenate([coords[...], noise[...]], axis=0)
    three = split3(stacked)
    small[...] = jnp.concatenate(
        [p.astype(F32) for p in three] + [jnp.zeros((LANES - 12, points), F32)], axis=0
    ).astype(BF16)
    ranks = rank_row[...]
    chunk = 256

    def permute(step, carry):
        at = pl.multiple_of(step * chunk, chunk)
        want = (lax.broadcasted_iota(jnp.int32, (chunk, 1), 0) + at).astype(F32)
        onehot = jnp.where(ranks == want, 1.0, 0.0).astype(BF16)
        moved = jnp.dot(onehot, pieces[...], preferred_element_type=F32)
        sorted_values[pl.ds(at, chunk), :] = moved[:, :LANES] + moved[:, LANES:]
        got = lax.dot_general(onehot, small[...], (((1,), (1,)), ((), ())), preferred_element_type=F32)
        got = (got + pltpu.roll(got, LANES - 4, 1)) + pltpu.roll(got, LANES - 8, 1)
        flat = jnp.transpose(got)
        lanes[0:4, pl.ds(at, chunk)] = flat[0:4, :]
        for k in range(4):
            scale = 4.0 if k < 3 else 1.0
            rows[k, pl.ds(at, chunk), :] = jnp.broadcast_to(got[:, k : k + 1] * scale, (chunk, LANES))
        return carry

    lax.fori_loop(0, points // chunk, permute, 0)
    for k in range(4):
        rows[k, points:, :] = jnp.full((ROWS, LANES), FAR if k < 3 else 0.0, F32)
    lanes[4:5, :] = jnp.full((1, points), jnp.min(coords[0:1, :]), F32)
    lanes[5:6, :] = jnp.full((1, points), jnp.max(coords[0:1, :]), F32)
    lanes[6:8, :] = jnp.ones((2, points), F32)


def sort_points(coords, noise, values):
    points, width = values.shape
    return pl.pallas_call(
        functools.partial(sort_kernel, points),
        out_shape=(
            jax.ShapeDtypeStruct((points, width), F32),
            jax.ShapeDtypeStruct((8, points), F32),
            pltpu.VMEM((4, points + ROWS, LANES), F32),
            jax.ShapeDtypeStruct((1, points), F32),
            jax.ShapeDtypeStruct((points, LANES), F32),
        ),
        in_specs=[vmem_spec()] * 3,
        out_specs=[vmem_spec()] * 5,
        scratch_shapes=[
            pltpu.VMEM((points, LANES), F32),
            pltpu.VMEM((points, 2 * LANES), BF16),
            pltpu.VMEM((LANES, points), BF16),
        ],
        compiler_params=pltpu.CompilerParams(vmem_limit_bytes=20 * MIB),
        name="sort_points",
    )(coords, noise, values)


def tile_values(rows, cols, at, count):
    tcol, xcol, ycol = cols
    span = pl.ds(at, count)
    dtime = jnp.abs(rows[0, span, :] - tcol)
    dx = rows[1, span, :] - xcol
    dy = rows[2, span, :] - ycol
    square = jnp.maximum(dx * dx + dy * dy, 1e-30)
    dist = square * lax.rsqrt(square)
    near = jnp.maximum(4.0 - dtime, 0.0) * jnp.maximum(4.0 - dist, 0.0)
    near = near * near
    return near * near * ((dtime + 1.0) * (dist + 1.0))


def window_cols(lanes, half, offset):
    groups = []
    for g in range(WINDOW // LANES):
        at = pl.multiple_of(offset + g * LANES, LANES)
        groups.append([lanes[half, k : k + 1, pl.ds(at, LANES)] * 4.0 for k in range(3)])
    return groups


def fill_tile(tile, rows, groups, at):
    for part in range(ROWS // 16):
        for g, cols in enumerate(groups):
            start = pl.multiple_of(at + part * 16, 16)
            high, low = split2(tile_values(rows, cols, start, 16))
            tile[part * 16 : (part + 1) * 16, g * LANES : (g + 1) * LANES] = high
            tile[part * 16 : (part + 1) * 16, WINDOW + g * LANES : WINDOW + (g + 1) * LANES] = low


def eval_kernel(windows, per_half, ranges, lanes, rows, cache):
    def window(w, slot):
        half = w // per_half
        offset = (w % per_half) * WINDOW
        first = ranges[0, w]
        blocks = ranges[1, w]
        groups = window_cols(lanes, half, offset)

        def block(b, carry):
            @pl.when(slot + b < SLOTS)
            def _():
                at = pl.multiple_of(first + b * ROWS, 16)
                fill_tile(cache.at[slot + b], rows, groups, at)

            return carry

        lax.fori_loop(0, blocks, block, 0)
        return slot + blocks

    lax.fori_loop(0, windows, window, 0)


def eval_slab(ranges, lanes, rows):
    points = lanes.shape[2]
    per_half = points // WINDOW
    windows = 2 * per_half
    return pl.pallas_call(
        functools.partial(eval_kernel, windows, per_half),
        out_shape=pltpu.VMEM((SLOTS, ROWS, 2 * WINDOW), BF16),
        in_specs=[smem_spec(), vmem_spec(), vmem_spec()],
        out_specs=vmem_spec(),
        compiler_params=pltpu.CompilerParams(vmem_limit_bytes=8 * MIB),
        cost_estimate=pl.CostEstimate(flops=60_000_000, bytes_accessed=20_000_000, transcendentals=0),
        name="eval_slab",
    )(ranges, lanes, rows)


def product_kernel(windows, per_half, points, ranges, lanes, rows, cache, values, before, out, acc, doubled, tile):
    acc[...] = jnp.zeros_like(acc)

    def window(w, slot):
        half = w // per_half
        offset = pl.multiple_of((w % per_half) * WINDOW, WINDOW)
        first = ranges[0, w]
        blocks = ranges[1, w]

        @pl.when(blocks > 0)
        def _():
            high, low = split2(values[half, pl.ds(offset, WINDOW), :])
            doubled[0:WINDOW, 0:LANES] = high
            doubled[0:WINDOW, LANES : 2 * LANES] = low
            doubled[WINDOW : 2 * WINDOW, 0:LANES] = high
            doubled[WINDOW : 2 * WINDOW, LANES : 2 * LANES] = low

        def block(b, carry):
            at = pl.multiple_of(first + b * ROWS, 16)

            @pl.when(slot + b < SLOTS)
            def _():
                acc[pl.ds(at, ROWS), :] += jnp.dot(
                    cache[slot + b], doubled[...], preferred_element_type=F32
                )

            @pl.when(slot + b >= SLOTS)
            def _():
                fill_tile(tile, rows, window_cols(lanes, half, offset), at)
                acc[pl.ds(at, ROWS), :] += jnp.dot(tile[...], doubled[...], preferred_element_type=F32)

            return carry

        lax.fori_loop(0, blocks, block, 0)
        return slot + blocks

    lax.fori_loop(0, windows, window, 0)
    total = acc[0:points, 0:LANES] + acc[0:points, LANES : 2 * LANES]
    out[...] = before[...] + total * (2.0**-16)


def own_kernel(windows, per_half, points, ranges, lanes, rows, cache, values, out, acc, doubled, tile):
    class Before:
        def __getitem__(self, index):
            return rows[3, 0:points, :] * values[0]

    product_kernel(windows, per_half, points, ranges, lanes, rows, cache, values, Before(), out, acc, doubled, tile)


def product_slab(ranges, lanes, rows, cache, values, before):
    points = lanes.shape[2]
    per_half = points // WINDOW
    windows = 2 * per_half
    body = own_kernel if before is None else product_kernel
    extra = () if before is None else (before,)
    return pl.pallas_call(
        functools.partial(body, windows, per_half, points),
        out_shape=jax.ShapeDtypeStruct((points, LANES), F32),
        in_specs=[smem_spec()] + [vmem_spec()] * (4 + len(extra)),
        out_specs=vmem_spec(),
        scratch_shapes=[
            pltpu.VMEM((points + ROWS, 2 * LANES), F32),
            pltpu.VMEM((2 * WINDOW, 2 * LANES), BF16),
            pltpu.VMEM((ROWS, 2 * WINDOW), BF16),
        ],
        compiler_params=pltpu.CompilerParams(vmem_limit_bytes=16 * MIB),
        cost_estimate=pl.CostEstimate(flops=2_000_000_000, bytes_accessed=10_000_000, transcendentals=0),
        name="product_slab",
    )(ranges, lanes, rows, cache, values, *extra)


def unsort_into(points, rank_col, source, pieces, emit):
    high, low = split2(source[...])
    pieces[:, 0:LANES] = high
    pieces[:, LANES : 2 * LANES] = low
    chunk = 256

    def step(index, carry):
        at = pl.multiple_of(index * chunk, chunk)
        ranks = rank_col[pl.ds(at, chunk), :]
        lane = lax.broadcasted_iota(jnp.int32, (chunk, LANES), 1).astype(F32)
        onehot = jnp.concatenate(
            [jnp.where(ranks - float(g * LANES) == lane, 1.0, 0.0).astype(BF16) for g in range(points // LANES)],
            axis=1,
        )
        moved = jnp.dot(onehot, pieces[...], preferred_element_type=F32)
        return emit(at, chunk, moved[:, :LANES] + moved[:, LANES:], carry)

    zero = jnp.zeros((8, LANES), F32)
    return lax.fori_loop(0, points // chunk, step, (zero, zero))


def fold(value):
    return jnp.sum(value.reshape(value.shape[0] // 8, 8, LANES), axis=0)


def first_kernel(points, rank_col, source, anomalies, image, sums, pieces):
    def emit(at, chunk, moved, carry):
        given = anomalies[pl.ds(at, chunk), :]
        image[pl.ds(at, chunk), :] = moved
        return carry[0] + fold(given * given), carry[1] + fold(given * moved)

    square, curve = unsort_into(points, rank_col, source, pieces, emit)
    sums[0:1, :] = jnp.sum(square, axis=0, keepdims=True)
    sums[1:2, :] = jnp.sum(curve, axis=0, keepdims=True)
    sums[2:8, :] = jnp.zeros((6, LANES), F32)


def second_kernel(points, rank_col, source, anomalies, image, scalars, second, sums, pieces):
    alpha = scalars[0:1, :]
    more = 1.0 + scalars[1:2, :]

    def emit(at, chunk, moved, carry):
        given = anomalies[pl.ds(at, chunk), :]
        once = image[pl.ds(at, chunk), :]
        second[pl.ds(at, chunk), :] = moved
        direction = more * given - alpha * once
        turned = more * once - alpha * moved
        return carry[0] + fold(direction * turned), carry[1]

    curve, _ = unsort_into(points, rank_col, source, pieces, emit)
    sums[...] = jnp.zeros((8, LANES), F32)
    sums[0:1, :] = jnp.sum(curve, axis=0, keepdims=True)


def unsort(body, *operands):
    points = operands[0].shape[0]
    return pl.pallas_call(
        functools.partial(body, points),
        out_shape=(
            jax.ShapeDtypeStruct((points, LANES), F32),
            jax.ShapeDtypeStruct((8, LANES), F32),
        ),
        in_specs=[vmem_spec()] * len(operands),
        out_specs=[vmem_spec()] * 2,
        scratch_shapes=[pltpu.VMEM((points, 2 * LANES), BF16)],
        compiler_params=pltpu.CompilerParams(vmem_limit_bytes=16 * MIB),
        cost_estimate=pl.CostEstimate(flops=4_000_000_000, bytes_accessed=5_000_000, transcendentals=0),
        name="unsort",
    )(*operands)


def pair_swap(block):
    count = lax.axis_size("tm")
    return lax.ppermute(block, "tm", [(i, i ^ 1) for i in range(count)])


def pair_shift(block):
    count = lax.axis_size("tm")
    route = []
    for i in range(count):
        source = i - 2 if i % 2 == 0 else i + 2
        if 0 <= source < count:
            route.append((source, i))
    return lax.ppermute(block, "tm", route)


def core_swap(block):
    count = lax.axis_size("tile")
    return lax.ppermute(block, "tile", [(i, i ^ 1) for i in range(count)])


def gather_slabs(block):
    partner = core_swap(block)
    near = pair_swap(block)
    far = pair_shift(near)
    return (
        jnp.stack([block, partner]),
        jnp.stack([near, core_swap(near)]),
        jnp.stack([far, core_swap(far)]),
    )


def gather_small(block):
    tms, tiles = lax.axis_size("tm"), lax.axis_size("tile")

    def fetch(offset, flip):
        route = []
        for t in range(tms):
            source = offset(t)
            if 0 <= source < tms:
                for c in range(tiles):
                    route.append((source * tiles + (c ^ flip), t * tiles + c))
        return lax.ppermute(block, ("tm", "tile"), route)

    near = lambda t: t ^ 1
    far = lambda t: t - 1 if t % 2 == 0 else t + 1
    return (
        jnp.stack([block, fetch(lambda t: t, 1)]),
        jnp.stack([fetch(near, 0), fetch(near, 1)]),
        jnp.stack([fetch(far, 0), fetch(far, 1)]),
    )


def total(value):
    count = lax.axis_size("tm")
    value = value + core_swap(value)
    step = 1
    while step < count:
        value = value + lax.ppermute(value, "tm", [(i, i ^ step) for i in range(count)])
        step *= 2
    return value


def find_ranges(rows, lanes):
    points = rows.shape[1]
    x = rows[1]
    cols = lanes[:, 1, :].reshape(-1, WINDOW)
    low, high = cols[:, 0], cols[:, -1]
    per_half = points // WINDOW
    begin = jnp.sum((low[:, None] - x[None, :] >= 1.0).astype(jnp.int32), axis=1)
    end = points - jnp.sum((x[None, :] - high[:, None] >= 1.0).astype(jnp.int32), axis=1)
    apart = jnp.logical_or(lanes[:, 4, 0] - rows[5, 0] >= 1.0, rows[4, 0] - lanes[:, 5, 0] >= 1.0)
    reach = jnp.logical_and(jnp.logical_not(apart), lanes[:, 6, 0] > 0.5)
    reach = jnp.logical_and(jnp.repeat(reach, per_half), end > begin)
    first = begin // 16 * 16
    blocks = (end - first + ROWS - 1) // ROWS
    return jnp.stack([first, jnp.where(reach, blocks, 0)])


def local(coords, anomalies, noise_var):
    sorted_values, lanes, rows, _, rank_col = sort_points(coords, noise_var[None, :], anomalies)
    lane_slabs = gather_small(lanes)
    value_slabs = gather_slabs(sorted_values)
    ranges = [find_ranges(lanes, slab) for slab in lane_slabs]
    caches = [eval_slab(r, slab, rows) for r, slab in zip(ranges, lane_slabs)]

    def apply(values):
        image = None
        for k in range(3):
            image = product_slab(ranges[k], lane_slabs[k], rows, caches[k], values[k], image)
        return image

    image = apply(value_slabs)
    image_slabs = gather_slabs(image)
    image0, sums = unsort(first_kernel, rank_col, image, anomalies)
    sums = total(sums)
    rr0 = sums[0:1]
    alpha0 = rr0 / sums[1:2]
    residual = anomalies - alpha0 * image0
    rr1 = total(jnp.broadcast_to(jnp.sum(residual * residual, axis=0, keepdims=True), (8, LANES)))[0:1]
    beta = rr1 / rr0
    scalars = jnp.concatenate([alpha0, beta, jnp.zeros((6, LANES), F32)], axis=0)
    twice = apply(image_slabs)
    image1, curve = unsort(second_kernel, rank_col, twice, anomalies, image0, scalars)
    alpha1 = rr1 / total(curve)[0:1]
    weights = (alpha0 + alpha1 * (1.0 + beta)) * anomalies - (alpha1 * alpha0) * image0
    turned = (1.0 + beta) * image0 - alpha0 * image1
    return weights, residual - alpha1 * turned


def solution(mesh):
    placed = (
        P(None, ("region", "tm", "tile")),
        P(("region", "tm", "tile"), None),
        P(("region", "tm", "tile")),
    )
    return jax.shard_map(
        local,
        mesh=mesh,
        in_specs=placed,
        out_specs=(P(("region", "tm", "tile"), None), P(("region", "tm", "tile"), None)),
        check_vma=False,
    )
```

```python
import functools

import jax
import jax.numpy as jnp
from jax import lax
from jax.experimental import pallas as pl
from jax.experimental.pallas import tpu as pltpu
from jax.sharding import PartitionSpec as P

LANES = 128
ROWS = 224
SLOTS = 72
UNROLL = 4
CHUNKS = 2
FAR = 1.0e6
F32 = jnp.float32
BF16 = jnp.bfloat16
MIB = 1 << 20


def vmem_spec():
    return pl.BlockSpec(memory_space=pltpu.VMEM)


def smem_spec():
    return pl.BlockSpec(memory_space=pltpu.SMEM)


def split2(value):
    high = value.astype(BF16)
    low = (value - high.astype(F32)).astype(BF16)
    return high, low


def list_length(points):
    return 2 * (points // LANES) * -(-points // ROWS) + UNROLL


def sort_kernel(points, coords, noise, values, *refs):
    out_values, (lanes, rows, ranks, xcol, facts, sorted_facts, sorted_values, rank_row, rank_smem, sem) = (
        refs[:CHUNKS],
        refs[CHUNKS:],
    )
    groups = points // LANES
    for g in range(groups):
        here = slice(g * LANES, (g + 1) * LANES)
        xcol[here, :] = jnp.transpose(jnp.broadcast_to(coords[1:2, here], (LANES, LANES)))

    xrow = [jnp.broadcast_to(coords[1:2, g * LANES : (g + 1) * LANES], (8, LANES)) for g in range(groups)]
    lane = lax.broadcasted_iota(jnp.int32, (8, LANES), 1)
    sub = lax.broadcasted_iota(jnp.int32, (8, LANES), 0)
    counts = tuple(jnp.zeros((8, LANES), F32) for _ in range(groups))
    for jg in range(groups):

        def count(step, carry):
            at = pl.multiple_of(jg * LANES + step * 8, 8)
            mine = xcol[pl.ds(at, 8), :]
            out = []
            for ig in range(groups):
                if ig == jg:
                    before = jnp.logical_or(
                        mine < xrow[ig],
                        jnp.logical_and(mine == xrow[ig], sub + step * 8 < lane),
                    )
                elif ig > jg:
                    before = mine <= xrow[ig]
                else:
                    before = mine < xrow[ig]
                out.append(carry[ig] + jnp.where(before, 1.0, 0.0))
            return tuple(out)

        counts = lax.fori_loop(0, LANES // 8, count, counts, unroll=2)
    for g in range(groups):
        rank_row[0:1, g * LANES : (g + 1) * LANES] = jnp.sum(counts[g], axis=0, keepdims=True).astype(jnp.int32)
    ranks[...] = rank_row[...]
    copy = pltpu.make_async_copy(rank_row, rank_smem, sem)
    copy.start()
    blank = jnp.zeros((LANES - 4, LANES), F32)
    for g in range(groups):
        here = slice(g * LANES, (g + 1) * LANES)
        facts[here, :] = jnp.transpose(jnp.concatenate([coords[:, here], noise[:, here], blank], axis=0))
    copy.wait()
    size = points // CHUNKS

    def scatter(step, carry):
        at = pl.multiple_of(step * 8, 8)
        block = values[pl.ds(at, 8), :]
        fact = facts[pl.ds(at, 8), :]
        for k in range(8):
            to = rank_smem[0, at + k]
            sorted_facts[pl.ds(to, 1), :] = fact[k : k + 1, :]
            sorted_values[pl.ds(to, 1), :] = block[k : k + 1, :]
        return carry

    lax.fori_loop(0, points // 8, scatter, 0, unroll=4)
    for c in range(CHUNKS):
        out_values[c][...] = sorted_values[c * size : (c + 1) * size, :]
    for g in range(groups):
        here = slice(g * LANES, (g + 1) * LANES)
        got = sorted_facts[here, :]
        lanes[0:4, here] = jnp.transpose(got)[0:4, :]
        for k in range(4):
            scale = 4.0 if k < 3 else 1.0
            rows[k, here, :] = jnp.broadcast_to(got[:, k : k + 1] * scale, (LANES, LANES))
    for k in range(4):
        rows[k, points:, :] = jnp.full((ROWS, LANES), FAR if k < 3 else 0.0, F32)
    lanes[4:5, :] = jnp.full((1, points), jnp.min(coords[0:1, :]), F32)
    lanes[5:6, :] = jnp.full((1, points), jnp.max(coords[0:1, :]), F32)
    lanes[6:8, :] = jnp.ones((2, points), F32)


def sort_points(coords, noise, values):
    points, width = values.shape
    out = pl.pallas_call(
        functools.partial(sort_kernel, points),
        out_shape=tuple(jax.ShapeDtypeStruct((points // CHUNKS, width), F32) for _ in range(CHUNKS))
        + (
            jax.ShapeDtypeStruct((8, points), F32),
            pltpu.VMEM((4, points + ROWS, LANES), F32),
            jax.ShapeDtypeStruct((1, points), jnp.int32),
        ),
        in_specs=[vmem_spec()] * 3,
        out_specs=[vmem_spec()] * (CHUNKS + 3),
        scratch_shapes=[
            pltpu.VMEM((points, LANES), F32),
            pltpu.VMEM((points, LANES), F32),
            pltpu.VMEM((points, LANES), F32),
            pltpu.VMEM((points, LANES), F32),
            pltpu.VMEM((1, points), jnp.int32),
            pltpu.SMEM((1, points), jnp.int32),
            pltpu.SemaphoreType.DMA,
        ],
        compiler_params=pltpu.CompilerParams(vmem_limit_bytes=16 * MIB),
        name="sort_points",
    )(coords, noise, values)
    return out[:CHUNKS], *out[CHUNKS:]


def tile_values(rows, cols, at, count):
    span = pl.ds(at, count)
    dtime = jnp.abs(rows[0, span, :] - cols[0])
    dx = rows[1, span, :] - cols[1]
    dy = rows[2, span, :] - cols[2]
    square = jnp.maximum(dx * dx + dy * dy, 1e-30)
    dist = square * lax.rsqrt(square)
    near = jnp.maximum(4.0 - dtime, 0.0) * jnp.maximum(4.0 - dist, 0.0)
    near = near * near
    return near * near * ((dtime + 1.0) * (dist + 1.0))


def fill_tile(tile, rows, facts, at):
    cols = [jnp.broadcast_to(facts[k : k + 1, :] * 4.0, (16, LANES)) for k in range(3)]
    for part in range(ROWS // 16):
        start = pl.multiple_of(at + part * 16, 16)
        high, low = split2(tile_values(rows, cols, start, 16))
        tile[part * 16 : (part + 1) * 16, 0:LANES] = high
        tile[part * 16 : (part + 1) * 16, LANES:] = low


def find_ranges(points, own, lanes, table, base):
    windows = points // LANES
    x = jnp.concatenate([lanes[1:2, g * LANES : (g + 1) * LANES] for g in range(windows)], axis=0)
    low = jnp.broadcast_to(x[:, 0:1], (windows, LANES))
    high = jnp.broadcast_to(x[:, LANES - 1 : LANES], (windows, LANES))
    begin = jnp.zeros((windows, LANES), F32)
    beyond = jnp.zeros((windows, LANES), F32)
    for g in range(windows):
        row = jnp.broadcast_to(own[1:2, g * LANES : (g + 1) * LANES], (windows, LANES))
        begin = begin + jnp.where(low - row >= 1.0, 1.0, 0.0)
        beyond = beyond + jnp.where(row - high >= 1.0, 1.0, 0.0)
    begin = jnp.sum(begin, axis=1, keepdims=True)
    end = points - jnp.sum(beyond, axis=1, keepdims=True)
    first = begin.astype(jnp.int32) // 16 * 16
    length = end - first.astype(F32)
    blocks = jnp.zeros((windows, 1), F32)
    for k in range(-(-points // ROWS)):
        blocks = blocks + jnp.where(length > float(k * ROWS), 1.0, 0.0)
    apart = jnp.maximum(lanes[4:5, 0:1] - own[5:6, 0:1], own[4:5, 0:1] - lanes[5:6, 0:1])
    apart = jnp.where(lanes[6:7, 0:1] > 0.5, apart, 2.0)
    blocks = jnp.where(jnp.logical_and(end > begin, jnp.broadcast_to(apart, (windows, 1)) < 1.0), blocks, 0.0)
    table[base : base + windows, 0:LANES] = jnp.broadcast_to(first, (windows, LANES))
    table[base : base + windows, LANES:] = jnp.broadcast_to(blocks.astype(jnp.int32), (windows, LANES))


def eval_kernel(points, own, lanes_a, lanes_b, rows, cache, work, facts, table, table_smem, sem):
    windows = points // LANES
    for half, lanes in enumerate((lanes_a, lanes_b)):
        find_ranges(points, own, lanes, table, half * windows)
    copy = pltpu.make_async_copy(table, table_smem, sem)
    copy.start()
    for half, lanes in enumerate((lanes_a, lanes_b)):
        for g in range(windows):
            facts[half * windows + g] = lanes[:, g * LANES : (g + 1) * LANES]
    copy.wait()

    def window(w, slot):
        first = table_smem[w, 0]
        blocks = table_smem[w, LANES]

        def block(b, carry):
            work[0, slot + b] = first + b * ROWS
            work[1, slot + b] = w
            return carry

        lax.fori_loop(0, blocks, block, 0)
        return slot + blocks

    total = lax.fori_loop(0, 2 * windows, window, 0)
    for k in range(UNROLL):
        work[0, total + k] = points
        work[1, total + k] = 0
    work[2, 0] = total

    def slot(s, carry):
        fill_tile(cache.at[s], rows, facts[work[1, s]], pl.multiple_of(work[0, s], 16))
        return carry

    lax.fori_loop(0, jnp.minimum(total, SLOTS), slot, 0)


def eval_pair(own, lanes, rows):
    points = own.shape[1]
    windows = points // LANES
    return pl.pallas_call(
        functools.partial(eval_kernel, points),
        out_shape=(
            pltpu.VMEM((SLOTS, ROWS, 2 * LANES), BF16),
            jax.ShapeDtypeStruct((3, list_length(points)), jnp.int32),
        ),
        in_specs=[vmem_spec()] * 4,
        out_specs=(vmem_spec(), smem_spec()),
        scratch_shapes=[
            pltpu.VMEM((2 * windows, 8, LANES), F32),
            pltpu.VMEM((2 * windows, 2 * LANES), jnp.int32),
            pltpu.SMEM((2 * windows, 2 * LANES), jnp.int32),
            pltpu.SemaphoreType.DMA,
        ],
        compiler_params=pltpu.CompilerParams(vmem_limit_bytes=4 * MIB),
        cost_estimate=pl.CostEstimate(flops=6_000_000_000, bytes_accessed=200_000, transcendentals=0),
        name="eval_pair",
    )(own, *lanes, rows)


def product_kernel(points, start, extra, work, lanes_a, lanes_b, rows, cache, *refs):
    values, refs = refs[: 2 * CHUNKS], refs[2 * CHUNKS :]
    before, refs = refs[: 0 if start else CHUNKS], refs[0 if start else CHUNKS :]
    inputs, refs = refs[: extra[1]], refs[extra[1] :]
    out, refs = refs[:CHUNKS], refs[CHUNKS:]
    sums, refs = refs[: extra[2]], refs[extra[2] :]
    acc, pairs, tile = refs
    windows = points // LANES
    size = points // CHUNKS
    per_chunk = size // LANES
    total = work[2, 0]
    acc[...] = jnp.zeros_like(acc)

    @pl.when(total > 0)
    def _():
        for piece in range(2 * CHUNKS):

            def split(w, carry):
                high, low = split2(values[piece][pl.ds(pl.multiple_of(w * LANES, LANES), LANES), :])
                both = jnp.concatenate([high, low], axis=1)
                pairs[piece * per_chunk + w, 0:LANES, :] = both
                pairs[piece * per_chunk + w, LANES:, :] = both
                return carry

            lax.fori_loop(0, per_chunk, split, 0)

        def slots(step, carry):
            for k in range(UNROLL):
                s = step * UNROLL + k
                at = pl.multiple_of(work[0, s], 16)
                acc[pl.ds(at, ROWS), :] += jnp.dot(
                    cache[s], pairs[work[1, s]], preferred_element_type=F32
                )
            return carry

        kept = jnp.minimum(total, SLOTS)
        lax.fori_loop(0, (kept + UNROLL - 1) // UNROLL, slots, 0)

        def again(s, carry):
            at = pl.multiple_of(work[0, s], 16)
            w = work[1, s]
            offset = pl.multiple_of(lax.rem(w, windows) * LANES, LANES)
            in_first = w < windows
            facts = jnp.where(in_first, lanes_a[:, pl.ds(offset, LANES)], lanes_b[:, pl.ds(offset, LANES)])
            fill_tile(tile, rows, facts, at)
            acc[pl.ds(at, ROWS), :] += jnp.dot(tile[...], pairs[w], preferred_element_type=F32)
            return carry

        lax.fori_loop(SLOTS, total, again, 0)

    marks = [jnp.zeros((8, LANES), F32)] * 2
    for c in range(CHUNKS):
        here = slice(c * size, (c + 1) * size)
        image = (acc[here, 0:LANES] + acc[here, LANES:]) * (2.0**-16)
        if start:
            image = image + rows[3, here, :] * values[c][...]
        else:
            image = image + before[c][...]
        out[c][...] = image
        if extra[0] is not None:
            marks = extra[0](c, image, inputs, marks)
    if extra[2]:
        sums[0][...] = jnp.zeros((8, LANES), F32)
        for k in range(2):
            sums[0][k : k + 1, :] = jnp.sum(marks[k], axis=0, keepdims=True)


def fold(value):
    return jnp.sum(value.reshape(value.shape[0] // 8, 8, LANES), axis=0)


def first_marks(c, image, inputs, marks):
    given = inputs[c][...]
    return [marks[0] + fold(given * given), marks[1] + fold(given * image)]


def second_marks(c, image, inputs, marks):
    given, once, scalars = inputs[c][...], inputs[CHUNKS + c][...], inputs[2 * CHUNKS]
    alpha, more = scalars[0:1, :], 1.0 + scalars[1:2, :]
    direction = more * given - alpha * once
    turned = more * once - alpha * image
    return [marks[0] + fold(direction * turned), marks[1]]


def product_pair(work, lanes, rows, cache, values, before, marks=None, inputs=()):
    points = lanes[0].shape[1]
    windows = points // LANES
    start = before is None
    before = () if start else before
    operands = (*lanes, rows, cache, *values[0], *values[1], *before, *inputs)
    has_sums = marks is not None
    out = pl.pallas_call(
        functools.partial(product_kernel, points, start, (marks, len(inputs), int(has_sums))),
        out_shape=[jax.ShapeDtypeStruct((points // CHUNKS, LANES), F32)] * CHUNKS
        + [jax.ShapeDtypeStruct((8, LANES), F32)] * has_sums,
        in_specs=[smem_spec()] + [vmem_spec()] * len(operands),
        out_specs=[vmem_spec()] * (CHUNKS + has_sums),
        scratch_shapes=[
            pltpu.VMEM((points + ROWS, 2 * LANES), F32),
            pltpu.VMEM((2 * windows, 2 * LANES, 2 * LANES), BF16),
            pltpu.VMEM((ROWS, 2 * LANES), BF16),
        ],
        compiler_params=pltpu.CompilerParams(vmem_limit_bytes=18 * MIB),
        cost_estimate=pl.CostEstimate(flops=4_000_000_000, bytes_accessed=4_000_000, transcendentals=0),
        name="product_pair",
    )(work, *operands)
    return (tuple(out[:CHUNKS]), out[CHUNKS]) if has_sums else tuple(out)


def unsort_kernel(points, ranks, *refs):
    source, (out, stage) = refs[:CHUNKS], refs[CHUNKS:]
    size = points // CHUNKS
    for c in range(CHUNKS):
        stage[c * size : (c + 1) * size, :] = source[c][...]

    def gather(step, carry):
        at = pl.multiple_of(step * 8, 8)
        out[pl.ds(at, 8), :] = jnp.concatenate(
            [stage[pl.ds(ranks[0, at + k], 1), :] for k in range(8)], axis=0
        )
        return carry

    lax.fori_loop(0, points // 8, gather, 0, unroll=4)


def unsort(ranks, source):
    points = ranks.shape[1]
    return pl.pallas_call(
        functools.partial(unsort_kernel, points),
        out_shape=jax.ShapeDtypeStruct((points, LANES), F32),
        in_specs=[smem_spec()] + [vmem_spec()] * CHUNKS,
        out_specs=vmem_spec(),
        scratch_shapes=[pltpu.VMEM((points, LANES), F32)],
        compiler_params=pltpu.CompilerParams(vmem_limit_bytes=8 * MIB),
        cost_estimate=pl.CostEstimate(flops=3_000_000_000, bytes_accessed=2_000_000, transcendentals=0),
        name="unsort",
    )(ranks, *source)


def pair_swap(block):
    count = lax.axis_size("tm")
    return lax.ppermute(block, "tm", [(i, i ^ 1) for i in range(count)])


def pair_shift(block):
    count = lax.axis_size("tm")
    route = []
    for i in range(count):
        source = i - 2 if i % 2 == 0 else i + 2
        if 0 <= source < count:
            route.append((source, i))
    return lax.ppermute(block, "tm", route)


def core_swap(block):
    count = lax.axis_size("tile")
    return lax.ppermute(block, "tile", [(i, i ^ 1) for i in range(count)])


def gather_pairs(chunks):
    near = tuple(pair_swap(c) for c in chunks)
    partner = tuple(core_swap(c) for c in chunks)
    far = tuple(pair_shift(c) for c in near)
    near_partner = tuple(core_swap(c) for c in near)
    far_partner = tuple(core_swap(c) for c in far)
    return (chunks, partner), (near, near_partner), (far, far_partner)


def gather_small(block):
    tms, tiles = lax.axis_size("tm"), lax.axis_size("tile")

    def fetch(offset, flip):
        route = []
        for t in range(tms):
            source = offset(t)
            if 0 <= source < tms:
                for c in range(tiles):
                    route.append((source * tiles + (c ^ flip), t * tiles + c))
        return lax.ppermute(block, ("tm", "tile"), route)

    near = lambda t: t ^ 1
    far = lambda t: t - 1 if t % 2 == 0 else t + 1
    return (block, fetch(lambda t: t, 1)), (fetch(near, 0), fetch(near, 1)), (fetch(far, 0), fetch(far, 1))


def total(value):
    count = lax.axis_size("tm")
    value = value + core_swap(value)
    step = 1
    while step < count:
        value = value + lax.ppermute(value, "tm", [(i, i ^ step) for i in range(count)])
        step *= 2
    return value


def local(coords, anomalies, noise_var):
    given, lanes, rows, ranks = sort_points(coords, noise_var[None, :], anomalies)
    lane_pairs = gather_small(lanes)
    value_pairs = gather_pairs(given)
    evals = [eval_pair(lanes, pair, rows) for pair in lane_pairs]

    def apply(values, marks, inputs):
        image = None
        for k in range(3):
            last = dict(marks=marks, inputs=inputs) if k == 2 else {}
            image = product_pair(evals[k][1], lane_pairs[k], rows, evals[k][0], values[k], image, **last)
        return image

    once, sums = apply(value_pairs, first_marks, given)
    once_pairs = gather_pairs(once)
    image0 = unsort(ranks, once)
    sums = total(sums)
    rr0 = sums[0:1]
    alpha0 = rr0 / sums[1:2]
    squares = sum(jnp.sum(jnp.square(g - alpha0 * o), axis=0, keepdims=True) for g, o in zip(given, once))
    rr1 = total(jnp.broadcast_to(squares, (8, LANES)))[0:1]
    beta = rr1 / rr0
    scalars = jnp.concatenate([alpha0, beta, jnp.zeros((6, LANES), F32)], axis=0)
    twice, curve = apply(once_pairs, second_marks, (*given, *once, scalars))
    image1 = unsort(ranks, twice)
    alpha1 = rr1 / total(curve)[0:1]
    weights = (alpha0 + alpha1 * (1.0 + beta)) * anomalies - (alpha1 * alpha0) * image0
    turned = (1.0 + beta) * image0 - alpha0 * image1
    return weights, (anomalies - alpha0 * image0) - alpha1 * turned


def solution(mesh):
    placed = (
        P(None, ("region", "tm", "tile")),
        P(("region", "tm", "tile"), None),
        P(("region", "tm", "tile")),
    )
    return jax.shard_map(
        local,
        mesh=mesh,
        in_specs=placed,
        out_specs=(P(("region", "tm", "tile"), None), P(("region", "tm", "tile"), None)),
        check_vma=False,
    )
```

```python
import functools

import jax
import jax.numpy as jnp
from jax import lax
from jax.experimental import pallas as pl
from jax.experimental.pallas import tpu as pltpu
from jax.sharding import PartitionSpec as P

LANES = 128
ROWS = 224
SLOTS = 72
UNROLL = 8
EVAL_UNROLL = 2
PIECES = 2
FAR = 1.0e6
F32 = jnp.float32
BF16 = jnp.bfloat16
MIB = 1 << 20


def vmem_spec():
    return pl.BlockSpec(memory_space=pltpu.VMEM)


def smem_spec():
    return pl.BlockSpec(memory_space=pltpu.SMEM)


def split2(value):
    high = value.astype(BF16)
    low = (value - high.astype(F32)).astype(BF16)
    return high, low


def list_length(points):
    return 2 * (points // LANES) * -(-points // ROWS) + UNROLL


def header_rows(points):
    return -(-(3 * (points // LANES) + 3) // 8) * 8


def piece_sizes(points):
    large = points // LANES * 5 // 8 * LANES
    return [large, points - large]


def spans(chunks, top):
    found, start = [], 0
    for c, chunk in enumerate(chunks):
        skip = top if c == 0 else 0
        found.append((chunk, start, skip, chunk.shape[0] - skip))
        start += chunk.shape[0] - skip
    return found


def group_rows(chunks, top, start):
    for chunk, begin, skip, size in spans(chunks, top):
        if begin <= start < begin + size:
            return chunk, slice(start - begin + skip, start - begin + skip + LANES)
    raise ValueError(start)


def read_rows(chunks, top, start):
    chunk, here = group_rows(chunks, top, start)
    return chunk[here, :]


def sort_kernel(points, coords_hbm, noise_hbm, values_hbm, *refs):
    out_values, refs = refs[: PIECES + 1], refs[PIECES + 1 :]
    rows, ranks, coords, noise, values, xcol, facts, sorted_facts, sorted_values, rank_row, rank_smem, sems = refs
    fetches = [
        pltpu.make_async_copy(source, target, sems.at[k])
        for k, (source, target) in enumerate(((coords_hbm, coords), (noise_hbm, noise), (values_hbm, values)))
    ]
    for fetch in fetches:
        fetch.start()
    fetches[0].wait()
    groups = points // LANES
    for g in range(groups):
        here = slice(g * LANES, (g + 1) * LANES)
        xcol[here, :] = jnp.transpose(jnp.broadcast_to(coords[1:2, here], (LANES, LANES)))

    xrow = [jnp.broadcast_to(coords[1:2, g * LANES : (g + 1) * LANES], (8, LANES)) for g in range(groups)]
    lane = lax.broadcasted_iota(jnp.int32, (8, LANES), 1)
    sub = lax.broadcasted_iota(jnp.int32, (8, LANES), 0)
    counts = tuple(jnp.zeros((8, LANES), F32) for _ in range(groups))
    for jg in range(groups):

        def count(step, carry):
            at = pl.multiple_of(jg * LANES + step * 8, 8)
            mine = xcol[pl.ds(at, 8), :]
            out = []
            for ig in range(groups):
                if ig == jg:
                    before = jnp.logical_or(
                        mine < xrow[ig],
                        jnp.logical_and(mine == xrow[ig], sub + step * 8 < lane),
                    )
                elif ig > jg:
                    before = mine <= xrow[ig]
                else:
                    before = mine < xrow[ig]
                out.append(carry[ig] + jnp.where(before, 1.0, 0.0))
            return tuple(out)

        counts = lax.fori_loop(0, LANES // 8, count, counts, unroll=2)
    for g in range(groups):
        rank_row[0:1, g * LANES : (g + 1) * LANES] = jnp.sum(counts[g], axis=0, keepdims=True).astype(jnp.int32)
    ranks[...] = rank_row[...]
    copy = pltpu.make_async_copy(rank_row, rank_smem, sems.at[3])
    copy.start()
    fetches[1].wait()
    blank = jnp.zeros((LANES - 4, LANES), F32)
    for g in range(groups):
        here = slice(g * LANES, (g + 1) * LANES)
        facts[here, :] = jnp.transpose(jnp.concatenate([coords[:, here], noise[:, here], blank], axis=0))
    copy.wait()
    fetches[2].wait()

    def scatter(step, carry):
        at = pl.multiple_of(step * 8, 8)
        block = values[pl.ds(at, 8), :]
        fact = facts[pl.ds(at, 8), :]
        for k in range(8):
            to = rank_smem[0, at + k]
            sorted_facts[pl.ds(to, 1), :] = fact[k : k + 1, :]
            sorted_values[pl.ds(to, 1), :] = block[k : k + 1, :]
        return carry

    lax.fori_loop(0, points // 8, scatter, 0, unroll=4)
    header = header_rows(points)
    whole = out_values[PIECES]
    whole[header:, :] = sorted_values[...]
    for chunk, start, skip, size in spans(out_values[:PIECES], header):
        chunk[skip:, :] = sorted_values[start : start + size, :]
    head = out_values[0]
    for g in range(groups):
        here = slice(g * LANES, (g + 1) * LANES)
        got = sorted_facts[here, :]
        flat = jnp.transpose(got)
        for k in range(4):
            if k < 3:
                head[k * groups + g : k * groups + g + 1, :] = flat[k : k + 1, :]
            scale = 4.0 if k < 3 else 1.0
            rows[k, here, :] = jnp.broadcast_to(got[:, k : k + 1] * scale, (LANES, LANES))
    for k in range(4):
        rows[k, points:, :] = jnp.full((ROWS, LANES), FAR if k < 3 else 0.0, F32)
    end = 3 * groups
    head[end : end + 1, :] = jnp.full((1, LANES), jnp.min(coords[0:1, :]), F32)
    head[end + 1 : end + 2, :] = jnp.full((1, LANES), jnp.max(coords[0:1, :]), F32)
    head[end + 2 : header, :] = jnp.ones((header - end - 2, LANES), F32)
    whole[0:header, :] = head[0:header, :]


def sort_points(coords, noise, values):
    points, width = values.shape
    header = header_rows(points)
    out = pl.pallas_call(
        functools.partial(sort_kernel, points),
        out_shape=tuple(
            jax.ShapeDtypeStruct((size + (header if c in (0, PIECES) else 0), width), F32)
            for c, size in enumerate([*piece_sizes(points), points])
        )
        + (
            pltpu.VMEM((4, points + ROWS, LANES), F32),
            jax.ShapeDtypeStruct((1, points), jnp.int32),
        ),
        in_specs=[pl.BlockSpec(memory_space=pltpu.HBM)] * 3,
        out_specs=[vmem_spec()] * (PIECES + 3),
        scratch_shapes=[
            pltpu.VMEM((3, points), F32),
            pltpu.VMEM((1, points), F32),
            pltpu.VMEM((points, width), F32),
            pltpu.VMEM((points, LANES), F32),
            pltpu.VMEM((points, LANES), F32),
            pltpu.VMEM((points, LANES), F32),
            pltpu.VMEM((points, LANES), F32),
            pltpu.VMEM((1, points), jnp.int32),
            pltpu.SMEM((1, points), jnp.int32),
            pltpu.SemaphoreType.DMA((4,)),
        ],
        compiler_params=pltpu.CompilerParams(vmem_limit_bytes=14 * MIB),
        name="sort_points",
    )(coords, noise, values)
    return out[:PIECES], *out[PIECES:]


def tile_values(rows, cols, at, count):
    span = pl.ds(at, count)
    dtime = jnp.abs(rows[0, span, :] - cols[0])
    dx = rows[1, span, :] - cols[1]
    dy = rows[2, span, :] - cols[2]
    square = jnp.maximum(dx * dx + dy * dy, 1e-30)
    dist = square * lax.rsqrt(square)
    near = jnp.maximum(4.0 - dtime, 0.0) * jnp.maximum(4.0 - dist, 0.0)
    near = near * near
    return near * near * ((dtime + 1.0) * (dist + 1.0))


def fill_tile(tile, rows, facts, w, step, at):
    cols = [jnp.broadcast_to(facts[pl.ds(k * step + w, 1), :], (16, LANES)) for k in range(3)]
    for part in range(ROWS // 16):
        start = pl.multiple_of(at + part * 16, 16)
        high, low = split2(tile_values(rows, cols, start, 16))
        tile[part * 16 : (part + 1) * 16, 0:LANES] = high
        tile[part * 16 : (part + 1) * 16, LANES:] = low


def gather_facts(windows, facts, heads):
    for half, head in enumerate(heads):
        for k in range(3):
            base = (2 * k + half) * windows
            facts[base : base + windows, :] = head[k * windows : (k + 1) * windows, :] * 4.0


def find_ranges(points, own, other, table, base):
    windows = points // LANES
    end_row = 3 * windows
    x = other[windows : 2 * windows, :]
    low = jnp.broadcast_to(x[:, 0:1], (windows, LANES))
    high = jnp.broadcast_to(x[:, LANES - 1 : LANES], (windows, LANES))
    begin = jnp.zeros((windows, LANES), F32)
    beyond = jnp.zeros((windows, LANES), F32)
    for g in range(windows):
        row = jnp.broadcast_to(own[windows + g : windows + g + 1, :], (windows, LANES))
        begin = begin + jnp.where(low - row >= 1.0, 1.0, 0.0)
        beyond = beyond + jnp.where(row - high >= 1.0, 1.0, 0.0)
    begin = jnp.sum(begin, axis=1, keepdims=True)
    end = points - jnp.sum(beyond, axis=1, keepdims=True)
    first = begin.astype(jnp.int32) // 16 * 16
    length = end - first.astype(F32)
    blocks = jnp.zeros((windows, 1), F32)
    for k in range(-(-points // ROWS)):
        blocks = blocks + jnp.where(length > float(k * ROWS), 1.0, 0.0)
    early, late, mark = end_row, end_row + 1, end_row + 2
    apart = jnp.maximum(
        other[early : early + 1, 0:1] - own[late : late + 1, 0:1],
        own[early : early + 1, 0:1] - other[late : late + 1, 0:1],
    )
    apart = jnp.where(other[mark : mark + 1, 0:1] > 0.5, apart, 2.0)
    blocks = jnp.where(jnp.logical_and(end > begin, jnp.broadcast_to(apart, (windows, 1)) < 1.0), blocks, 0.0)
    table[base : base + windows, 0:LANES] = jnp.broadcast_to(first, (windows, LANES))
    table[base : base + windows, LANES:] = jnp.broadcast_to(blocks.astype(jnp.int32), (windows, LANES))


def eval_kernel(points, own, head_a, head_b, rows, cache, work, facts, table, table_smem, sem):
    windows = points // LANES
    for half, head in enumerate((head_a, head_b)):
        find_ranges(points, own, head, table, half * windows)
    copy = pltpu.make_async_copy(table, table_smem, sem)
    copy.start()
    gather_facts(windows, facts, (head_a, head_b))
    copy.wait()

    def window(w, slot):
        first = table_smem[w, 0]
        blocks = table_smem[w, LANES]

        def block(b, carry):
            work[0, slot + b] = first + b * ROWS
            work[1, slot + b] = w
            return carry

        lax.fori_loop(0, blocks, block, 0)
        return slot + blocks

    total = lax.fori_loop(0, 2 * windows, window, 0)
    for k in range(UNROLL):
        work[0, total + k] = points
        work[1, total + k] = 0
    work[2, 0] = total

    def slots(step, carry):
        for k in range(EVAL_UNROLL):
            s = step * EVAL_UNROLL + k
            fill_tile(cache.at[s], rows, facts, work[1, s], 2 * windows, pl.multiple_of(work[0, s], 16))
        return carry

    kept = jnp.minimum(total, SLOTS)
    lax.fori_loop(0, (kept + EVAL_UNROLL - 1) // EVAL_UNROLL, slots, 0)


def eval_pair(points, own, heads, rows):
    windows = points // LANES
    return pl.pallas_call(
        functools.partial(eval_kernel, points),
        out_shape=(
            pltpu.VMEM((SLOTS, ROWS, 2 * LANES), BF16),
            jax.ShapeDtypeStruct((3, list_length(points)), jnp.int32),
            jax.ShapeDtypeStruct((6 * windows, LANES), F32),
        ),
        in_specs=[vmem_spec()] * 4,
        out_specs=(vmem_spec(), smem_spec(), vmem_spec()),
        scratch_shapes=[
            pltpu.VMEM((2 * windows, 2 * LANES), jnp.int32),
            pltpu.SMEM((2 * windows, 2 * LANES), jnp.int32),
            pltpu.SemaphoreType.DMA,
        ],
        compiler_params=pltpu.CompilerParams(vmem_limit_bytes=4 * MIB),
        cost_estimate=pl.CostEstimate(flops=1_000_000, bytes_accessed=100_000, transcendentals=0),
        name="eval_pair",
    )(own, *heads, rows)


def product_kernel(points, headed, counts, marker, work, facts, rows, cache, *refs):
    groups = []
    for count in counts:
        groups.append(refs[:count])
        refs = refs[count:]
    first, second, before, given, once, out, sums = groups
    values = (first, second)
    acc, pairs, tile = refs
    windows = points // LANES
    header = header_rows(points)
    top = header if headed else 0
    total = work[2, 0]
    acc[...] = jnp.zeros_like(acc)

    @pl.when(total > 0)
    def _():
        for half in range(2):
            for chunk, start, skip, size in spans(values[half], top):
                base = half * windows + start // LANES

                def split(w, carry):
                    high, low = split2(chunk[pl.ds(pl.multiple_of(skip + w * LANES, 8), LANES), :])
                    both = jnp.concatenate([high, low], axis=1)
                    pairs[base + w, 0:LANES, :] = both
                    pairs[base + w, LANES:, :] = both
                    return carry

                lax.fori_loop(0, size // LANES, split, 0)

        def slots(step, carry):
            for k in range(UNROLL):
                s = step * UNROLL + k
                at = pl.multiple_of(work[0, s], 16)
                acc[pl.ds(at, ROWS), :] += jnp.dot(
                    cache[s], pairs[work[1, s]], preferred_element_type=F32
                )
            return carry

        kept = jnp.minimum(total, SLOTS)
        lax.fori_loop(0, (kept + UNROLL - 1) // UNROLL, slots, 0)

        @pl.when(total > SLOTS)
        def _():
            def again(s, carry):
                at = pl.multiple_of(work[0, s], 16)
                w = work[1, s]
                fill_tile(tile, rows, facts, w, 2 * windows, at)
                acc[pl.ds(at, ROWS), :] += jnp.dot(tile[...], pairs[w], preferred_element_type=F32)
                return carry

            lax.fori_loop(SLOTS, total, again, 0)

    marks = [jnp.zeros((8, LANES), F32)] * 5
    for start in range(0, points, LANES):
        here = slice(start, start + LANES)
        image = (acc[here, 0:LANES] + acc[here, LANES:]) * (2.0**-16)
        if before:
            image = image + read_rows(before, 0, start)
        else:
            image = image + rows[3, here, :] * read_rows(first, top, start)
        if len(out) > 1:
            target, place = group_rows(out[:-1], 0, start)
            target[place, :] = image
        out[-1][here, :] = image
        if marker is not None:
            marks = marker(marks, image, read_rows(given, header, start), read_rows(once, 0, start))
    if marker is not None:
        sums[0][...] = jnp.zeros((8, LANES), F32)
        for k in range(5):
            sums[0][k : k + 1, :] = jnp.sum(marks[k], axis=0, keepdims=True)


def fold(value):
    return jnp.sum(value.reshape(value.shape[0] // 8, 8, LANES), axis=0)


def inner_sums(marks, image, given, once):
    terms = (given * given, given * once, once * once, given * image, once * image)
    return [mark + fold(term) for mark, term in zip(marks, terms)]


def product_pair(points, evaluated, rows, values, headed, before=(), sent=False, marker=None, given=(), once=()):
    cache, work, facts = evaluated
    windows = points // LANES
    groups = (*values, before, given, once)
    operands = (facts, rows, cache, *(x for group in groups for x in group))
    sizes = [*(piece_sizes(points) if sent else []), points]
    sums = int(marker is not None)
    counts = [len(group) for group in groups] + [len(sizes), sums]
    out = pl.pallas_call(
        functools.partial(product_kernel, points, headed, counts, marker),
        out_shape=[jax.ShapeDtypeStruct((size, LANES), F32) for size in sizes]
        + [jax.ShapeDtypeStruct((8, LANES), F32)] * sums,
        in_specs=[smem_spec()] + [vmem_spec()] * len(operands),
        out_specs=[vmem_spec()] * (len(sizes) + sums),
        scratch_shapes=[
            pltpu.VMEM((points + ROWS, 2 * LANES), F32),
            pltpu.VMEM((2 * windows, 2 * LANES, 2 * LANES), BF16),
            pltpu.VMEM((ROWS, 2 * LANES), BF16),
        ],
        compiler_params=pltpu.CompilerParams(vmem_limit_bytes=15 * MIB),
        cost_estimate=pl.CostEstimate(flops=1_000_000, bytes_accessed=100_000, transcendentals=0),
        name="product_pair",
    )(work, *operands)
    return tuple(out)


def unsort_kernel(points, ranks, source, out):
    def gather(step, carry):
        at = pl.multiple_of(step * 8, 8)
        out[pl.ds(at, 8), :] = jnp.concatenate(
            [source[pl.ds(ranks[0, at + k], 1), :] for k in range(8)], axis=0
        )
        return carry

    lax.fori_loop(0, points // 8, gather, 0, unroll=4)


def unsort(ranks, source):
    points = ranks.shape[1]
    return pl.pallas_call(
        functools.partial(unsort_kernel, points),
        out_shape=jax.ShapeDtypeStruct((points, LANES), F32),
        in_specs=[smem_spec(), vmem_spec()],
        out_specs=vmem_spec(),
        compiler_params=pltpu.CompilerParams(vmem_limit_bytes=8 * MIB),
        cost_estimate=pl.CostEstimate(flops=1_000_000, bytes_accessed=100_000, transcendentals=0),
        name="unsort",
    )(ranks, source)


def pair_swap(block):
    count = lax.axis_size("tm")
    return lax.ppermute(block, "tm", [(i, i ^ 1) for i in range(count)])


def pair_shift(block, turn=0):
    count = lax.axis_size("tm")
    route = []
    for i in range(count):
        source = i - 2 if i % 2 == turn else i + 2
        if 0 <= source < count:
            route.append((source, i))
    return lax.ppermute(block, "tm", route)


def core_swap(block):
    count = lax.axis_size("tile")
    return lax.ppermute(block, "tile", [(i, i ^ 1) for i in range(count)])


def after(value, *earlier):
    return lax.optimization_barrier((value, *earlier))[0]


def stride_sum(value, step):
    count = lax.axis_size("tm")
    return value + lax.ppermute(value, "tm", [(i, i ^ step) for i in range(count)])


def far_strides():
    step, steps = 2, []
    while step < lax.axis_size("tm"):
        steps.append(step)
        step *= 2
    return steps


def total(value):
    for step in [1] + far_strides():
        value = stride_sum(value, step)
    return value + core_swap(value)


def local(coords, anomalies, noise_var):
    points = anomalies.shape[0]
    operands = [pltpu.with_memory_space_constraint(x, pltpu.HBM) for x in (coords, noise_var[None, :], anomalies)]
    given, whole, rows, ranks = sort_points(*operands)

    near = [pair_swap(c) for c in given]
    turned = pair_shift(given[1], 1)
    mates = core_swap(whole)
    own_eval = eval_pair(points, given[0], (given[0], mates), rows)
    image = product_pair(points, own_eval, rows, (given, (after(mates, own_eval[1]),)), True)
    near[0] = after(near[0], image[0], turned)
    far = [pair_shift(near[0])]
    near_mates = [core_swap(near[0])]
    near_eval = eval_pair(points, given[0], (near[0], near_mates[0]), rows)
    near[1] = after(near[1], near_eval[1])
    far.append(pair_swap(after(turned, near[1])))
    near_mates.append(core_swap(near[1]))
    image = product_pair(points, near_eval, rows, (near, near_mates), True, image)
    far[0] = after(far[0], image[0])
    far_mates = [core_swap(far[0])]
    far_eval = eval_pair(points, given[0], (far[0], far_mates[0]), rows)
    far[1] = after(far[1], far_eval[1])
    far_mates.append(core_swap(far[1]))
    *once, whole = product_pair(points, far_eval, rows, (far, far_mates), True, image, True)

    near = [pair_swap(c) for c in once]
    turned = pair_shift(once[1], 1)
    mates = core_swap(whole)
    image0 = unsort(ranks, after(whole, mates))
    image = product_pair(points, own_eval, rows, (once, (after(mates, image0),)), False)
    near[0] = after(near[0], image[0], turned)
    far = [pair_shift(near[0])]
    near_mates = [core_swap(near[0])]
    far.append(pair_swap(after(turned, near[1], near[0])))
    near_mates.append(core_swap(near[1]))
    image = product_pair(points, near_eval, rows, (near, near_mates), False, image)
    far_mates = [core_swap(c) for c in far]
    twice, sums = product_pair(points, far_eval, rows, (far, far_mates), False, image, False, inner_sums, given, once)
    image1 = unsort(ranks, twice)

    sums = total(sums)
    rr0, curve0, once_once, given_twice, once_twice = [sums[k : k + 1] for k in range(5)]
    alpha0 = rr0 / curve0
    rr1 = rr0 - 2.0 * alpha0 * curve0 + alpha0 * alpha0 * once_once
    beta = rr1 / rr0
    more = 1.0 + beta
    curve1 = more * more * curve0 - more * alpha0 * (given_twice + once_once) + alpha0 * alpha0 * once_twice
    alpha1 = rr1 / curve1
    residual = anomalies - alpha0 * image0
    weights = alpha0 * anomalies + alpha1 * (residual + beta * anomalies)
    again = (image0 - alpha0 * image1) + beta * image0
    return weights, residual - alpha1 * again


def solution(mesh):
    placed = (
        P(None, ("region", "tm", "tile")),
        P(("region", "tm", "tile"), None),
        P(("region", "tm", "tile")),
    )
    return jax.shard_map(
        local,
        mesh=mesh,
        in_specs=placed,
        out_specs=(P(("region", "tm", "tile"), None), P(("region", "tm", "tile"), None)),
        check_vma=False,
    )
```

```python
import functools

import jax
import jax.numpy as jnp
from jax import lax
from jax.experimental import pallas as pl
from jax.experimental.pallas import tpu as pltpu
from jax.sharding import PartitionSpec as P

LANES = 128
ROWS = 224
OWN_SLOTS = 72
SLOTS = 40
UNROLL = 8
EVAL_UNROLL = 2
PIECES = 2
FIRST_SHARE = 9
LATER_SHARE = 9
FAR = 1.0e6
F32 = jnp.float32
BF16 = jnp.bfloat16
MIB = 1 << 20


def vmem_spec():
    return pl.BlockSpec(memory_space=pltpu.VMEM)


def smem_spec():
    return pl.BlockSpec(memory_space=pltpu.SMEM)


def split2(value):
    high = value.astype(BF16)
    low = (value - high.astype(F32)).astype(BF16)
    return high, low


def list_length(points, halves):
    return halves * (points // LANES) * -(-points // ROWS) + UNROLL


def header_rows(points):
    return -(-(3 * (points // LANES) + 3) // 8) * 8


def piece_sizes(points, share):
    large = points // LANES * share // 16 * LANES
    return [large, points - large]


def spans(chunks, top):
    found, start = [], 0
    for c, chunk in enumerate(chunks):
        skip = top if c == 0 else 0
        found.append((chunk, start, skip, chunk.shape[0] - skip))
        start += chunk.shape[0] - skip
    return found


def group_rows(chunks, top, start):
    for chunk, begin, skip, size in spans(chunks, top):
        if begin <= start < begin + size:
            return chunk, slice(start - begin + skip, start - begin + skip + LANES)
    raise ValueError(start)


def read_rows(chunks, top, start):
    chunk, here = group_rows(chunks, top, start)
    return chunk[here, :]


def sort_kernel(points, coords_hbm, noise_hbm, values_hbm, *refs):
    out_values, refs = refs[: PIECES + 1], refs[PIECES + 1 :]
    rows, ranks, coords, noise, values, xcol, facts, sorted_facts, sorted_values, rank_row, rank_smem, sems = refs
    fetches = [
        pltpu.make_async_copy(source, target, sems.at[k])
        for k, (source, target) in enumerate(((coords_hbm, coords), (noise_hbm, noise), (values_hbm, values)))
    ]
    for fetch in fetches:
        fetch.start()
    fetches[0].wait()
    groups = points // LANES
    for g in range(groups):
        here = slice(g * LANES, (g + 1) * LANES)
        xcol[here, :] = jnp.transpose(jnp.broadcast_to(coords[1:2, here], (LANES, LANES)))

    xrow = [jnp.broadcast_to(coords[1:2, g * LANES : (g + 1) * LANES], (8, LANES)) for g in range(groups)]
    lane = lax.broadcasted_iota(jnp.int32, (8, LANES), 1)
    sub = lax.broadcasted_iota(jnp.int32, (8, LANES), 0)
    counts = tuple(jnp.zeros((8, LANES), F32) for _ in range(groups))
    for jg in range(groups):

        def count(step, carry):
            at = pl.multiple_of(jg * LANES + step * 8, 8)
            mine = xcol[pl.ds(at, 8), :]
            out = []
            for ig in range(groups):
                if ig == jg:
                    before = jnp.logical_or(
                        mine < xrow[ig],
                        jnp.logical_and(mine == xrow[ig], sub + step * 8 < lane),
                    )
                elif ig > jg:
                    before = mine <= xrow[ig]
                else:
                    before = mine < xrow[ig]
                out.append(carry[ig] + jnp.where(before, 1.0, 0.0))
            return tuple(out)

        counts = lax.fori_loop(0, LANES // 8, count, counts, unroll=2)
    for g in range(groups):
        rank_row[0:1, g * LANES : (g + 1) * LANES] = jnp.sum(counts[g], axis=0, keepdims=True).astype(jnp.int32)
    ranks[...] = rank_row[...]
    copy = pltpu.make_async_copy(rank_row, rank_smem, sems.at[3])
    copy.start()
    fetches[1].wait()
    blank = jnp.zeros((LANES - 4, LANES), F32)
    for g in range(groups):
        here = slice(g * LANES, (g + 1) * LANES)
        facts[here, :] = jnp.transpose(jnp.concatenate([coords[:, here], noise[:, here], blank], axis=0))
    copy.wait()
    fetches[2].wait()

    def scatter(step, carry):
        at = pl.multiple_of(step * 8, 8)
        block = values[pl.ds(at, 8), :]
        fact = facts[pl.ds(at, 8), :]
        for k in range(8):
            to = rank_smem[0, at + k]
            sorted_facts[pl.ds(to, 1), :] = fact[k : k + 1, :]
            sorted_values[pl.ds(to, 1), :] = block[k : k + 1, :]
        return carry

    lax.fori_loop(0, points // 8, scatter, 0, unroll=4)
    header = header_rows(points)
    whole = out_values[PIECES]
    whole[header:, :] = sorted_values[...]
    for chunk, start, skip, size in spans(out_values[:PIECES], header):
        chunk[skip:, :] = sorted_values[start : start + size, :]
    head = out_values[0]
    for g in range(groups):
        here = slice(g * LANES, (g + 1) * LANES)
        got = sorted_facts[here, :]
        flat = jnp.transpose(got)
        for k in range(4):
            if k < 3:
                head[k * groups + g : k * groups + g + 1, :] = flat[k : k + 1, :]
            scale = 4.0 if k < 3 else 1.0
            rows[k, here, :] = jnp.broadcast_to(got[:, k : k + 1] * scale, (LANES, LANES))
    for k in range(4):
        rows[k, points:, :] = jnp.full((ROWS, LANES), FAR if k < 3 else 0.0, F32)
    end = 3 * groups
    head[end : end + 1, :] = jnp.full((1, LANES), jnp.min(coords[0:1, :]), F32)
    head[end + 1 : end + 2, :] = jnp.full((1, LANES), jnp.max(coords[0:1, :]), F32)
    head[end + 2 : header, :] = jnp.ones((header - end - 2, LANES), F32)
    whole[0:header, :] = head[0:header, :]


def sort_points(coords, noise, values):
    points, width = values.shape
    header = header_rows(points)
    out = pl.pallas_call(
        functools.partial(sort_kernel, points),
        out_shape=tuple(
            jax.ShapeDtypeStruct((size + (header if c in (0, PIECES) else 0), width), F32)
            for c, size in enumerate([*piece_sizes(points, FIRST_SHARE), points])
        )
        + (
            pltpu.VMEM((4, points + ROWS, LANES), F32),
            jax.ShapeDtypeStruct((1, points), jnp.int32),
        ),
        in_specs=[pl.BlockSpec(memory_space=pltpu.HBM)] * 3,
        out_specs=[vmem_spec()] * (PIECES + 3),
        scratch_shapes=[
            pltpu.VMEM((3, points), F32),
            pltpu.VMEM((1, points), F32),
            pltpu.VMEM((points, width), F32),
            pltpu.VMEM((points, LANES), F32),
            pltpu.VMEM((points, LANES), F32),
            pltpu.VMEM((points, LANES), F32),
            pltpu.VMEM((points, LANES), F32),
            pltpu.VMEM((1, points), jnp.int32),
            pltpu.SMEM((1, points), jnp.int32),
            pltpu.SemaphoreType.DMA((4,)),
        ],
        compiler_params=pltpu.CompilerParams(vmem_limit_bytes=14 * MIB),
        name="sort_points",
    )(coords, noise, values)
    return out[:PIECES], *out[PIECES:]


def tile_values(rows, cols, at, count):
    span = pl.ds(at, count)
    dtime = jnp.abs(rows[0, span, :] - cols[0])
    dx = rows[1, span, :] - cols[1]
    dy = rows[2, span, :] - cols[2]
    square = jnp.maximum(dx * dx + dy * dy, 1e-30)
    dist = square * lax.rsqrt(square)
    near = jnp.maximum(4.0 - dtime, 0.0) * jnp.maximum(4.0 - dist, 0.0)
    near = near * near
    return near * near * ((dtime + 1.0) * (dist + 1.0))


def fill_tile(tile, rows, facts, w, step, at):
    cols = [jnp.broadcast_to(facts[pl.ds(k * step + w, 1), :], (16, LANES)) for k in range(3)]
    for part in range(ROWS // 16):
        start = pl.multiple_of(at + part * 16, 16)
        high, low = split2(tile_values(rows, cols, start, 16))
        tile[part * 16 : (part + 1) * 16, 0:LANES] = high
        tile[part * 16 : (part + 1) * 16, LANES:] = low


def gather_facts(windows, facts, heads):
    for half, head in enumerate(heads):
        for k in range(3):
            base = (len(heads) * k + half) * windows
            facts[base : base + windows, :] = head[k * windows : (k + 1) * windows, :] * 4.0


def find_ranges(points, own, other):
    windows = points // LANES
    early, late, mark = 3 * windows, 3 * windows + 1, 3 * windows + 2
    x = other[windows : 2 * windows, :]
    low = jnp.broadcast_to(x[:, 0:1], (windows, LANES))
    high = jnp.broadcast_to(x[:, LANES - 1 : LANES], (windows, LANES))
    begin = jnp.zeros((windows, LANES), F32)
    beyond = jnp.zeros((windows, LANES), F32)
    for g in range(windows):
        row = jnp.broadcast_to(own[windows + g : windows + g + 1, :], (windows, LANES))
        begin = begin + jnp.where(low - row >= 1.0, 1.0, 0.0)
        beyond = beyond + jnp.where(row - high >= 1.0, 1.0, 0.0)
    begin = jnp.sum(begin, axis=1, keepdims=True)
    end = points - jnp.sum(beyond, axis=1, keepdims=True)
    first = begin.astype(jnp.int32) // 16 * 16
    length = end - first.astype(F32)
    blocks = jnp.zeros((windows, 1), F32)
    for k in range(-(-points // ROWS)):
        blocks = blocks + jnp.where(length > float(k * ROWS), 1.0, 0.0)
    apart = jnp.maximum(
        other[early : early + 1, 0:1] - own[late : late + 1, 0:1],
        own[early : early + 1, 0:1] - other[late : late + 1, 0:1],
    )
    apart = jnp.where(other[mark : mark + 1, 0:1] > 0.5, apart, 2.0)
    blocks = jnp.where(jnp.logical_and(end > begin, jnp.broadcast_to(apart, (windows, 1)) < 1.0), blocks, 0.0)
    return jnp.broadcast_to(first * 64 + blocks.astype(jnp.int32), (windows, LANES))


def list_tiles(points, own, heads, work, facts, table, table_smem, sem):
    windows = points // LANES
    found = jnp.concatenate([find_ranges(points, own, head) for head in heads], axis=0)
    lane = lax.broadcasted_iota(jnp.int32, found.shape, 1)
    sub = lax.broadcasted_iota(jnp.int32, found.shape, 0)
    table[...] = jnp.sum(jnp.where(lane == sub, found, 0), axis=0, keepdims=True)
    copy = pltpu.make_async_copy(table, table_smem, sem)
    copy.start()
    gather_facts(windows, facts, heads)
    copy.wait()
    slot = jnp.int32(0)
    for w in range(len(heads) * windows):
        packed = table_smem[0, w]
        first = lax.shift_right_logical(packed, 6)
        blocks = lax.bitwise_and(packed, 63)
        for b in range(2):
            work[0, slot + b] = first + b * ROWS
            work[1, slot + b] = w

        @pl.when(blocks > 2)
        def _(slot=slot, first=first, blocks=blocks, w=w):
            def block(b, carry):
                work[0, slot + b] = first + b * ROWS
                work[1, slot + b] = w
                return carry

            lax.fori_loop(2, blocks, block, 0)

        slot = slot + blocks
    for k in range(UNROLL):
        work[0, slot + k] = points
        work[1, slot + k] = 0
    work[2, 0] = slot
    return slot


def keep_tiles(windows, work, facts, rows, cache, step):
    for k in range(EVAL_UNROLL):
        s = step * EVAL_UNROLL + k
        fill_tile(cache.at[s], rows, facts, work[1, s], windows, pl.multiple_of(work[0, s], 16))


def kept_shapes(points, halves, slots):
    return (
        pltpu.VMEM((slots, ROWS, 2 * LANES), BF16),
        jax.ShapeDtypeStruct((3, list_length(points, halves)), jnp.int32),
        jax.ShapeDtypeStruct((3 * halves * (points // LANES), LANES), F32),
    )


def list_scratch():
    return [pltpu.VMEM((1, LANES), jnp.int32), pltpu.SMEM((1, LANES), jnp.int32), pltpu.SemaphoreType.DMA]


def light_cost():
    return pl.CostEstimate(flops=1_000_000, bytes_accessed=100_000, transcendentals=0)


def split_values(points, values, top, pairs):
    for half, chunks in enumerate(values):
        for chunk, start, skip, size in spans(chunks, top):
            base = half * (points // LANES) + start // LANES

            def split(w, carry):
                high, low = split2(chunk[pl.ds(pl.multiple_of(skip + w * LANES, 8), LANES), :])
                both = jnp.concatenate([high, low], axis=1)
                pairs[base + w, 0:LANES, :] = both
                pairs[base + w, LANES:, :] = both
                return carry

            lax.fori_loop(0, size // LANES, split, 0)


def multiply(work, cache, pairs, acc, step, count):
    for k in range(count):
        s = step * count + k
        at = pl.multiple_of(work[0, s], 16)
        acc[pl.ds(at, ROWS), :] += jnp.dot(cache[s], pairs[work[1, s]], preferred_element_type=F32)


def multiply_rest(windows, work, facts, rows, cache, pairs, acc, tile, total):
    slots = cache.shape[0]

    @pl.when(total > slots)
    def _():
        def again(s, carry):
            at = pl.multiple_of(work[0, s], 16)
            w = work[1, s]
            fill_tile(tile, rows, facts, w, windows, at)
            acc[pl.ds(at, ROWS), :] += jnp.dot(tile[...], pairs[w], preferred_element_type=F32)
            return carry

        lax.fori_loop(slots, total, again, 0)


def finish(points, header, top, marker, rows, acc, groups):
    first, (before, given, once, out, sums) = groups[0], groups[-5:]
    marks = [jnp.zeros((8, LANES), F32)] * 5
    for start in range(0, points, LANES):
        here = slice(start, start + LANES)
        image = (acc[here, 0:LANES] + acc[here, LANES:]) * (2.0**-16)
        if before:
            image = image + read_rows(before, 0, start)
        else:
            image = image + rows[3, here, :] * read_rows(first, top, start)
        if len(out) > 1:
            target, place = group_rows(out[:-1], 0, start)
            target[place, :] = image
        out[-1][here, :] = image
        if marker is not None:
            marks = marker(marks, image, read_rows(given, header, start), read_rows(once, 0, start))
    if marker is not None:
        sums[0][...] = jnp.zeros((8, LANES), F32)
        for k in range(5):
            sums[0][k : k + 1, :] = jnp.sum(marks[k], axis=0, keepdims=True)


def take_groups(refs, counts):
    groups = []
    for count in counts:
        groups.append(refs[:count])
        refs = refs[count:]
    return groups, refs


def product_kernel(points, halves, headed, counts, marker, work, facts, rows, cache, *refs):
    groups, (acc, pairs, tile) = take_groups(refs, counts)
    header = header_rows(points)
    top = header if headed else 0
    total = work[2, 0]
    acc[...] = jnp.zeros_like(acc)

    @pl.when(total > 0)
    def _():
        split_values(points, groups[:halves], top, pairs)

        def slots(step, carry):
            multiply(work, cache, pairs, acc, step, UNROLL)
            return carry

        kept = jnp.minimum(total, cache.shape[0])
        lax.fori_loop(0, (kept + (UNROLL - 1)) // UNROLL, slots, 0)
        multiply_rest(halves * (points // LANES), work, facts, rows, cache, pairs, acc, tile, total)

    finish(points, header, top, marker, rows, acc, groups)


def both_kernel(points, halves, counts, own, rows, *refs):
    windows = halves * (points // LANES)
    groups, refs = take_groups(refs, counts)
    values = groups[:halves]
    cache, work, facts, acc, pairs, tile, table, table_smem, sem = refs
    header = header_rows(points)
    total = list_tiles(points, own, [half[0] for half in values], work, facts, table, table_smem, sem)
    acc[...] = jnp.zeros_like(acc)

    @pl.when(total > 0)
    def _():
        split_values(points, values, header, pairs)
        kept = jnp.minimum(total, cache.shape[0])
        steps = (kept + (EVAL_UNROLL - 1)) // EVAL_UNROLL
        keep_tiles(windows, work, facts, rows, cache, 0)

        def slots(step, carry):
            multiply(work, cache, pairs, acc, step - 1, EVAL_UNROLL)
            keep_tiles(windows, work, facts, rows, cache, step)
            return carry

        lax.fori_loop(1, steps, slots, 0)
        multiply(work, cache, pairs, acc, steps - 1, EVAL_UNROLL)
        multiply_rest(windows, work, facts, rows, cache, pairs, acc, tile, total)

    finish(points, header, header, None, rows, acc, groups)


def product_scratch(points, halves):
    return [
        pltpu.VMEM((points + ROWS, 2 * LANES), F32),
        pltpu.VMEM((halves * (points // LANES), 2 * LANES, 2 * LANES), BF16),
        pltpu.VMEM((ROWS, 2 * LANES), BF16),
    ]


def image_shapes(points, sent):
    sizes = [*(piece_sizes(points, LATER_SHARE) if sent else []), points]
    return [jax.ShapeDtypeStruct((size, LANES), F32) for size in sizes]


def fold(value):
    return jnp.sum(value.reshape(value.shape[0] // 8, 8, LANES), axis=0)


def all_sums(marks, image, given, once):
    terms = (given * given, given * once, once * once, given * image, once * image)
    return [mark + fold(term) for mark, term in zip(marks, terms)]


def product(points, evaluated, rows, values, before=(), marker=None, given=(), once=()):
    cache, work, facts = evaluated
    groups = (*values, before, given, once)
    operands = (facts, rows, cache, *(x for group in groups for x in group))
    sums = int(marker is not None)
    counts = [len(group) for group in groups] + [1, sums]
    out = pl.pallas_call(
        functools.partial(product_kernel, points, len(values), False, counts, marker),
        out_shape=image_shapes(points, False) + [jax.ShapeDtypeStruct((8, LANES), F32)] * sums,
        in_specs=[smem_spec()] + [vmem_spec()] * len(operands),
        out_specs=[vmem_spec()] * (1 + sums),
        scratch_shapes=product_scratch(points, len(values)),
        compiler_params=pltpu.CompilerParams(vmem_limit_bytes=15 * MIB),
        cost_estimate=light_cost(),
        name="product",
    )(work, *operands)
    return tuple(out)


def eval_product(points, own, rows, values, slots, before=(), sent=False):
    halves = len(values)
    groups = (*values, before, (), ())
    operands = (own, rows, *(x for group in groups for x in group))
    images = image_shapes(points, sent)
    counts = [len(group) for group in groups] + [len(images), 0]
    out = pl.pallas_call(
        functools.partial(both_kernel, points, halves, counts),
        out_shape=(*images, *kept_shapes(points, halves, slots)),
        in_specs=[vmem_spec()] * len(operands),
        out_specs=(*[vmem_spec()] * (len(images) + 1), smem_spec(), vmem_spec()),
        scratch_shapes=product_scratch(points, halves) + list_scratch(),
        compiler_params=pltpu.CompilerParams(vmem_limit_bytes=15 * MIB),
        cost_estimate=light_cost(),
        name="eval_product",
    )(*operands)
    return tuple(out[: len(images)]), tuple(out[len(images) :])


def unsort_kernel(points, ranks, source, out):
    def gather(step, carry):
        at = pl.multiple_of(step * 8, 8)
        out[pl.ds(at, 8), :] = jnp.concatenate(
            [source[pl.ds(ranks[0, at + k], 1), :] for k in range(8)], axis=0
        )
        return carry

    lax.fori_loop(0, points // 8, gather, 0, unroll=4)


def unsort(ranks, source):
    points = ranks.shape[1]
    return pl.pallas_call(
        functools.partial(unsort_kernel, points),
        out_shape=jax.ShapeDtypeStruct((points, LANES), F32),
        in_specs=[smem_spec(), vmem_spec()],
        out_specs=vmem_spec(),
        compiler_params=pltpu.CompilerParams(vmem_limit_bytes=8 * MIB),
        cost_estimate=light_cost(),
        name="unsort",
    )(ranks, source)


def pair_swap(block):
    count = lax.axis_size("tm")
    return lax.ppermute(block, "tm", [(i, i ^ 1) for i in range(count)])


def pair_shift(block, turn=0):
    count = lax.axis_size("tm")
    route = []
    for i in range(count):
        source = i - 2 if i % 2 == turn else i + 2
        if 0 <= source < count:
            route.append((source, i))
    return lax.ppermute(block, "tm", route)


def core_swap(block):
    count = lax.axis_size("tile")
    return lax.ppermute(block, "tile", [(i, i ^ 1) for i in range(count)])


def after(value, *earlier):
    return lax.optimization_barrier((value, *earlier))[0]


def stride_sum(value, step):
    count = lax.axis_size("tm")
    return value + lax.ppermute(value, "tm", [(i, i ^ step) for i in range(count)])


def far_strides():
    step, steps = 2, []
    while step < lax.axis_size("tm"):
        steps.append(step)
        step *= 2
    return steps


def total(value, beside):
    value = value + core_swap(value)
    steps = [1] + far_strides()
    for step in steps[:-1]:
        value = stride_sum(value, step)
    return stride_sum(after(value, beside), steps[-1])


def local(coords, anomalies, noise_var):
    points = anomalies.shape[0]
    operands = [pltpu.with_memory_space_constraint(x, pltpu.HBM) for x in (coords, noise_var[None, :], anomalies)]
    given, whole, rows, ranks = sort_points(*operands)

    near = [pair_swap(c) for c in given]
    turned = pair_shift(given[1], 1)
    mates = core_swap(whole)
    image, own_eval = eval_product(points, given[0], rows, (given, (mates,)), OWN_SLOTS)
    near[0] = after(near[0], image[0], turned)
    far = [pair_shift(near[0])]
    far.append(pair_swap(after(turned, near[1], near[0])))
    near_mates = [core_swap(c) for c in near]
    image, near_eval = eval_product(points, given[0], rows, (near,), SLOTS, image)
    far = [after(far[0], image[0], far[1]), far[1]]
    far_mates = [core_swap(c) for c in far]
    image, far_eval = eval_product(points, given[0], rows, (far,), SLOTS, image)
    (*once, whole), mate_eval = eval_product(points, given[0], rows, (near_mates, far_mates), SLOTS, image, True)

    near = [pair_swap(c) for c in once]
    turned = pair_shift(once[1], 1)
    mates = core_swap(whole)
    image0 = unsort(ranks, after(whole, mates))
    image = product(points, own_eval, rows, (once, (after(mates, image0),)))
    near[0] = after(near[0], image[0], turned)
    far = [pair_shift(near[0])]
    far.append(pair_swap(after(turned, near[1], near[0])))
    near_mates = [core_swap(c) for c in near]
    image = product(points, near_eval, rows, (near,), image)
    far_mates = [core_swap(far[0]), core_swap(after(far[1], image[0]))]
    image = product(points, far_eval, rows, (far,), image)
    twice, sums = product(points, mate_eval, rows, (near_mates, far_mates), image, all_sums, given, once)
    image1 = unsort(ranks, twice)

    sums = total(sums, image1)
    rr0, curve0, once_once, given_twice, once_twice = [sums[k : k + 1] for k in range(5)]
    alpha0 = rr0 / curve0
    rr1 = rr0 - 2.0 * alpha0 * curve0 + alpha0 * alpha0 * once_once
    beta = rr1 / rr0
    more = 1.0 + beta
    curve1 = more * more * curve0 - more * alpha0 * (given_twice + once_once) + alpha0 * alpha0 * once_twice
    alpha1 = rr1 / curve1
    residual = anomalies - alpha0 * image0
    weights = alpha0 * anomalies + alpha1 * (residual + beta * anomalies)
    again = (image0 - alpha0 * image1) + beta * image0
    return weights, residual - alpha1 * again


def solution(mesh):
    placed = (
        P(None, ("region", "tm", "tile")),
        P(("region", "tm", "tile"), None),
        P(("region", "tm", "tile")),
    )
    return jax.shard_map(
        local,
        mesh=mesh,
        in_specs=placed,
        out_specs=(P(("region", "tm", "tile"), None), P(("region", "tm", "tile"), None)),
        check_vma=False,
    )
```

```python
import functools

import jax
import jax.numpy as jnp
from jax import lax
from jax.experimental import pallas as pl
from jax.experimental.pallas import tpu as pltpu
from jax.sharding import PartitionSpec as P

LANES = 128
ROWS = 224
OWN_SLOTS = 72
SLOTS = 40
UNROLL = 8
EVAL_UNROLL = 2
FIRST_CUTS = (0, 10, 16)
LATER_CUTS = (0, 6, 12, 16)
FAR = 1.0e6
F32 = jnp.float32
BF16 = jnp.bfloat16
MIB = 1 << 20


def vmem_spec():
    return pl.BlockSpec(memory_space=pltpu.VMEM)


def smem_spec():
    return pl.BlockSpec(memory_space=pltpu.SMEM)


def split2(value):
    high = value.astype(BF16)
    low = (value - high.astype(F32)).astype(BF16)
    return high, low


def list_length(points, halves):
    return halves * (points // LANES) * -(-points // ROWS) + UNROLL


def header_rows(points):
    return -(-(3 * (points // LANES) + 3) // 8) * 8


def piece_sizes(points, cuts):
    rows = [points // LANES * cut // 16 * LANES for cut in cuts]
    return [b - a for a, b in zip(rows, rows[1:])]


def spans(chunks, top):
    found, start = [], 0
    for c, chunk in enumerate(chunks):
        skip = top if c == 0 else 0
        found.append((chunk, start, skip, chunk.shape[0] - skip))
        start += chunk.shape[0] - skip
    return found


def group_rows(chunks, top, start):
    for chunk, begin, skip, size in spans(chunks, top):
        if begin <= start < begin + size:
            return chunk, slice(start - begin + skip, start - begin + skip + LANES)
    raise ValueError(start)


def read_rows(chunks, top, start):
    chunk, here = group_rows(chunks, top, start)
    return chunk[here, :]


def sort_kernel(points, coords_hbm, noise_hbm, values_hbm, *refs):
    pieces = len(FIRST_CUTS) - 1
    out_values, refs = refs[: pieces + 1], refs[pieces + 1 :]
    rows, ranks, coords, noise, values, xcol, facts, sorted_facts, sorted_values, rank_row, rank_smem, sems = refs
    fetches = [
        pltpu.make_async_copy(source, target, sems.at[k])
        for k, (source, target) in enumerate(((coords_hbm, coords), (noise_hbm, noise), (values_hbm, values)))
    ]
    for fetch in fetches:
        fetch.start()
    fetches[0].wait()
    groups = points // LANES
    for g in range(groups):
        here = slice(g * LANES, (g + 1) * LANES)
        xcol[here, :] = jnp.transpose(jnp.broadcast_to(coords[1:2, here], (LANES, LANES)))

    xrow = [jnp.broadcast_to(coords[1:2, g * LANES : (g + 1) * LANES], (8, LANES)) for g in range(groups)]
    lane = lax.broadcasted_iota(jnp.int32, (8, LANES), 1)
    sub = lax.broadcasted_iota(jnp.int32, (8, LANES), 0)
    counts = tuple(jnp.zeros((8, LANES), F32) for _ in range(groups))
    for jg in range(groups):

        def count(step, carry):
            at = pl.multiple_of(jg * LANES + step * 8, 8)
            mine = xcol[pl.ds(at, 8), :]
            out = []
            for ig in range(groups):
                if ig == jg:
                    before = jnp.logical_or(
                        mine < xrow[ig],
                        jnp.logical_and(mine == xrow[ig], sub + step * 8 < lane),
                    )
                elif ig > jg:
                    before = mine <= xrow[ig]
                else:
                    before = mine < xrow[ig]
                out.append(carry[ig] + jnp.where(before, 1.0, 0.0))
            return tuple(out)

        counts = lax.fori_loop(0, LANES // 8, count, counts, unroll=2)
    for g in range(groups):
        rank_row[0:1, g * LANES : (g + 1) * LANES] = jnp.sum(counts[g], axis=0, keepdims=True).astype(jnp.int32)
    ranks[...] = rank_row[...]
    copy = pltpu.make_async_copy(rank_row, rank_smem, sems.at[3])
    copy.start()
    fetches[1].wait()
    blank = jnp.zeros((LANES - 4, LANES), F32)
    for g in range(groups):
        here = slice(g * LANES, (g + 1) * LANES)
        facts[here, :] = jnp.transpose(jnp.concatenate([coords[:, here], noise[:, here], blank], axis=0))
    copy.wait()
    fetches[2].wait()

    def scatter(step, carry):
        at = pl.multiple_of(step * 8, 8)
        block = values[pl.ds(at, 8), :]
        fact = facts[pl.ds(at, 8), :]
        for k in range(8):
            to = rank_smem[0, at + k]
            sorted_facts[pl.ds(to, 1), :] = fact[k : k + 1, :]
            sorted_values[pl.ds(to, 1), :] = block[k : k + 1, :]
        return carry

    lax.fori_loop(0, points // 8, scatter, 0, unroll=4)
    header = header_rows(points)
    whole = out_values[pieces]
    whole[header:, :] = sorted_values[...]
    for chunk, start, skip, size in spans(out_values[:pieces], header):
        chunk[skip:, :] = sorted_values[start : start + size, :]
    head = out_values[0]
    for g in range(groups):
        here = slice(g * LANES, (g + 1) * LANES)
        got = sorted_facts[here, :]
        flat = jnp.transpose(got)
        for k in range(4):
            if k < 3:
                head[k * groups + g : k * groups + g + 1, :] = flat[k : k + 1, :]
            scale = 4.0 if k < 3 else 1.0
            rows[k, here, :] = jnp.broadcast_to(got[:, k : k + 1] * scale, (LANES, LANES))
    for k in range(4):
        rows[k, points:, :] = jnp.full((ROWS, LANES), FAR if k < 3 else 0.0, F32)
    end = 3 * groups
    head[end : end + 1, :] = jnp.full((1, LANES), jnp.min(coords[0:1, :]), F32)
    head[end + 1 : end + 2, :] = jnp.full((1, LANES), jnp.max(coords[0:1, :]), F32)
    head[end + 2 : header, :] = jnp.ones((header - end - 2, LANES), F32)
    whole[0:header, :] = head[0:header, :]


def sort_points(coords, noise, values):
    points, width = values.shape
    header = header_rows(points)
    sizes = piece_sizes(points, FIRST_CUTS)
    out = pl.pallas_call(
        functools.partial(sort_kernel, points),
        out_shape=tuple(
            jax.ShapeDtypeStruct((size + (header if c in (0, len(sizes)) else 0), width), F32)
            for c, size in enumerate([*sizes, points])
        )
        + (
            pltpu.VMEM((4, points + ROWS, LANES), F32),
            jax.ShapeDtypeStruct((1, points), jnp.int32),
        ),
        in_specs=[pl.BlockSpec(memory_space=pltpu.HBM)] * 3,
        out_specs=[vmem_spec()] * (len(sizes) + 3),
        scratch_shapes=[
            pltpu.VMEM((3, points), F32),
            pltpu.VMEM((1, points), F32),
            pltpu.VMEM((points, width), F32),
            pltpu.VMEM((points, LANES), F32),
            pltpu.VMEM((points, LANES), F32),
            pltpu.VMEM((points, LANES), F32),
            pltpu.VMEM((points, LANES), F32),
            pltpu.VMEM((1, points), jnp.int32),
            pltpu.SMEM((1, points), jnp.int32),
            pltpu.SemaphoreType.DMA((4,)),
        ],
        compiler_params=pltpu.CompilerParams(vmem_limit_bytes=14 * MIB),
        name="sort_points",
    )(coords, noise, values)
    return out[: len(sizes)], *out[len(sizes) :]


def tile_values(rows, cols, at, count):
    span = pl.ds(at, count)
    dtime = jnp.abs(rows[0, span, :] - cols[0])
    dx = rows[1, span, :] - cols[1]
    dy = rows[2, span, :] - cols[2]
    square = jnp.maximum(dx * dx + dy * dy, 1e-30)
    dist = square * lax.rsqrt(square)
    near = jnp.maximum(4.0 - dtime, 0.0) * jnp.maximum(4.0 - dist, 0.0)
    near = near * near
    return near * near * ((dtime + 1.0) * (dist + 1.0))


def fill_tile(tile, rows, facts, w, step, at):
    cols = [jnp.broadcast_to(facts[pl.ds(k * step + w, 1), :], (16, LANES)) for k in range(3)]
    for part in range(ROWS // 16):
        start = pl.multiple_of(at + part * 16, 16)
        high, low = split2(tile_values(rows, cols, start, 16))
        tile[part * 16 : (part + 1) * 16, 0:LANES] = high
        tile[part * 16 : (part + 1) * 16, LANES:] = low


def gather_facts(windows, facts, heads):
    for half, head in enumerate(heads):
        for k in range(3):
            base = (len(heads) * k + half) * windows
            facts[base : base + windows, :] = head[k * windows : (k + 1) * windows, :] * 4.0


def find_ranges(points, own, other):
    windows = points // LANES
    early, late, mark = 3 * windows, 3 * windows + 1, 3 * windows + 2
    x = other[windows : 2 * windows, :]
    low = jnp.broadcast_to(x[:, 0:1], (windows, LANES))
    high = jnp.broadcast_to(x[:, LANES - 1 : LANES], (windows, LANES))
    begin = jnp.zeros((windows, LANES), F32)
    beyond = jnp.zeros((windows, LANES), F32)
    for g in range(windows):
        row = jnp.broadcast_to(own[windows + g : windows + g + 1, :], (windows, LANES))
        begin = begin + jnp.where(low - row >= 1.0, 1.0, 0.0)
        beyond = beyond + jnp.where(row - high >= 1.0, 1.0, 0.0)
    begin = jnp.sum(begin, axis=1, keepdims=True)
    end = points - jnp.sum(beyond, axis=1, keepdims=True)
    first = begin.astype(jnp.int32) // 16 * 16
    length = end - first.astype(F32)
    blocks = jnp.zeros((windows, 1), F32)
    for k in range(-(-points // ROWS)):
        blocks = blocks + jnp.where(length > float(k * ROWS), 1.0, 0.0)
    apart = jnp.maximum(
        other[early : early + 1, 0:1] - own[late : late + 1, 0:1],
        own[early : early + 1, 0:1] - other[late : late + 1, 0:1],
    )
    apart = jnp.where(other[mark : mark + 1, 0:1] > 0.5, apart, 2.0)
    blocks = jnp.where(jnp.logical_and(end > begin, jnp.broadcast_to(apart, (windows, 1)) < 1.0), blocks, 0.0)
    return jnp.broadcast_to(first * 64 + blocks.astype(jnp.int32), (windows, LANES))


def list_tiles(points, own, heads, work, facts, table, table_smem, sem, beside):
    windows = points // LANES
    found = jnp.concatenate([find_ranges(points, own, head) for head in heads], axis=0)
    lane = lax.broadcasted_iota(jnp.int32, found.shape, 1)
    sub = lax.broadcasted_iota(jnp.int32, found.shape, 0)
    table[...] = jnp.sum(jnp.where(lane == sub, found, 0), axis=0, keepdims=True)
    copy = pltpu.make_async_copy(table, table_smem, sem)
    copy.start()
    gather_facts(windows, facts, heads)
    beside()
    copy.wait()
    slot = jnp.int32(0)
    for w in range(len(heads) * windows):
        packed = table_smem[0, w]
        first = lax.shift_right_logical(packed, 6)
        blocks = lax.bitwise_and(packed, 63)
        for b in range(2):
            work[0, slot + b] = first + b * ROWS
            work[1, slot + b] = w

        @pl.when(blocks > 2)
        def _(slot=slot, first=first, blocks=blocks, w=w):
            def block(b, carry):
                work[0, slot + b] = first + b * ROWS
                work[1, slot + b] = w
                return carry

            lax.fori_loop(2, blocks, block, 0)

        slot = slot + blocks
    for k in range(UNROLL):
        work[0, slot + k] = points
        work[1, slot + k] = 0
    work[2, 0] = slot
    return slot


def keep_tiles(windows, work, facts, rows, cache, step):
    for k in range(EVAL_UNROLL):
        s = step * EVAL_UNROLL + k
        fill_tile(cache.at[s], rows, facts, work[1, s], windows, pl.multiple_of(work[0, s], 16))


def kept_shapes(points, halves, slots):
    return (
        pltpu.VMEM((slots, ROWS, 2 * LANES), BF16),
        jax.ShapeDtypeStruct((3, list_length(points, halves)), jnp.int32),
        jax.ShapeDtypeStruct((3 * halves * (points // LANES), LANES), F32),
    )


def list_scratch():
    return [pltpu.VMEM((1, LANES), jnp.int32), pltpu.SMEM((1, LANES), jnp.int32), pltpu.SemaphoreType.DMA]


def light_cost():
    return pl.CostEstimate(flops=1_000_000, bytes_accessed=100_000, transcendentals=0)


def split_values(points, values, top, pairs):
    for half, chunks in enumerate(values):
        for chunk, start, skip, size in spans(chunks, top):
            base = half * (points // LANES) + start // LANES

            def split(w, carry):
                high, low = split2(chunk[pl.ds(pl.multiple_of(skip + w * LANES, 8), LANES), :])
                both = jnp.concatenate([high, low], axis=1)
                pairs[base + w, 0:LANES, :] = both
                pairs[base + w, LANES:, :] = both
                return carry

            lax.fori_loop(0, size // LANES, split, 0)


def multiply(work, cache, pairs, acc, step, count):
    for k in range(count):
        s = step * count + k
        at = pl.multiple_of(work[0, s], 16)
        acc[pl.ds(at, ROWS), :] += jnp.dot(cache[s], pairs[work[1, s]], preferred_element_type=F32)


def multiply_rest(windows, work, facts, rows, cache, pairs, acc, tile, total):
    slots = cache.shape[0]

    @pl.when(total > slots)
    def _():
        def again(s, carry):
            at = pl.multiple_of(work[0, s], 16)
            w = work[1, s]
            fill_tile(tile, rows, facts, w, windows, at)
            acc[pl.ds(at, ROWS), :] += jnp.dot(tile[...], pairs[w], preferred_element_type=F32)
            return carry

        lax.fori_loop(slots, total, again, 0)


def finish(points, header, top, marker, rows, acc, groups):
    first, (before, given, once, out, sums) = groups[0], groups[-5:]
    marks = [jnp.zeros((8, LANES), F32)] * 5
    for start in range(0, points, LANES):
        here = slice(start, start + LANES)
        image = (acc[here, 0:LANES] + acc[here, LANES:]) * (2.0**-16)
        if before:
            image = image + read_rows(before, 0, start)
        else:
            image = image + rows[3, here, :] * read_rows(first, top, start)
        if len(out) > 1:
            target, place = group_rows(out[:-1], 0, start)
            target[place, :] = image
        out[-1][here, :] = image
        if marker is not None:
            marks = marker(marks, image, read_rows(given, header, start), read_rows(once, 0, start))
    if marker is not None:
        sums[0][...] = jnp.zeros((8, LANES), F32)
        for k in range(5):
            sums[0][k : k + 1, :] = jnp.sum(marks[k], axis=0, keepdims=True)


def take_groups(refs, counts):
    groups = []
    for count in counts:
        groups.append(refs[:count])
        refs = refs[count:]
    return groups, refs


def product_kernel(points, halves, headed, counts, marker, work, facts, rows, cache, *refs):
    groups, (acc, pairs, tile) = take_groups(refs, counts)
    header = header_rows(points)
    top = header if headed else 0
    total = work[2, 0]
    acc[...] = jnp.zeros_like(acc)

    @pl.when(total > 0)
    def _():
        split_values(points, groups[:halves], top, pairs)

        def slots(step, carry):
            multiply(work, cache, pairs, acc, step, UNROLL)
            return carry

        kept = jnp.minimum(total, cache.shape[0])
        lax.fori_loop(0, (kept + (UNROLL - 1)) // UNROLL, slots, 0)
        multiply_rest(halves * (points // LANES), work, facts, rows, cache, pairs, acc, tile, total)

    finish(points, header, top, marker, rows, acc, groups)


def both_kernel(points, halves, counts, own, rows, *refs):
    windows = halves * (points // LANES)
    groups, refs = take_groups(refs, counts)
    values = groups[:halves]
    cache, work, facts, acc, pairs, tile, table, table_smem, sem = refs
    header = header_rows(points)

    def prepare():
        acc[...] = jnp.zeros_like(acc)
        split_values(points, values, header, pairs)

    heads = [half[0] for half in values]
    total = list_tiles(points, own, heads, work, facts, table, table_smem, sem, prepare)

    @pl.when(total > 0)
    def _():
        kept = jnp.minimum(total, cache.shape[0])
        steps = (kept + (EVAL_UNROLL - 1)) // EVAL_UNROLL
        keep_tiles(windows, work, facts, rows, cache, 0)

        def slots(step, carry):
            multiply(work, cache, pairs, acc, step - 1, EVAL_UNROLL)
            keep_tiles(windows, work, facts, rows, cache, step)
            return carry

        lax.fori_loop(1, steps, slots, 0)
        multiply(work, cache, pairs, acc, steps - 1, EVAL_UNROLL)
        multiply_rest(windows, work, facts, rows, cache, pairs, acc, tile, total)

    finish(points, header, header, None, rows, acc, groups)


def product_scratch(points, halves):
    return [
        pltpu.VMEM((points + ROWS, 2 * LANES), F32),
        pltpu.VMEM((halves * (points // LANES), 2 * LANES, 2 * LANES), BF16),
        pltpu.VMEM((ROWS, 2 * LANES), BF16),
    ]


def image_shapes(points, sent):
    sizes = [*(piece_sizes(points, LATER_CUTS) if sent else []), points]
    return [jax.ShapeDtypeStruct((size, LANES), F32) for size in sizes]


def fold(value):
    return jnp.sum(value.reshape(value.shape[0] // 8, 8, LANES), axis=0)


def all_sums(marks, image, given, once):
    terms = (given * given, given * once, once * once, given * image, once * image)
    return [mark + fold(term) for mark, term in zip(marks, terms)]


def product(points, evaluated, rows, values, before=(), headed=False, marker=None, given=(), once=()):
    cache, work, facts = evaluated
    groups = (*values, before, given, once)
    operands = (facts, rows, cache, *(x for group in groups for x in group))
    sums = int(marker is not None)
    counts = [len(group) for group in groups] + [1, sums]
    out = pl.pallas_call(
        functools.partial(product_kernel, points, len(values), headed, counts, marker),
        out_shape=image_shapes(points, False) + [jax.ShapeDtypeStruct((8, LANES), F32)] * sums,
        in_specs=[smem_spec()] + [vmem_spec()] * len(operands),
        out_specs=[vmem_spec()] * (1 + sums),
        scratch_shapes=product_scratch(points, len(values)),
        compiler_params=pltpu.CompilerParams(vmem_limit_bytes=15 * MIB),
        cost_estimate=light_cost(),
        name="product",
    )(work, *operands)
    return tuple(out)


def eval_product(points, own, rows, values, slots, before=(), sent=False):
    halves = len(values)
    groups = (*values, before, (), ())
    operands = (own, rows, *(x for group in groups for x in group))
    images = image_shapes(points, sent)
    counts = [len(group) for group in groups] + [len(images), 0]
    out = pl.pallas_call(
        functools.partial(both_kernel, points, halves, counts),
        out_shape=(*images, *kept_shapes(points, halves, slots)),
        in_specs=[vmem_spec()] * len(operands),
        out_specs=(*[vmem_spec()] * (len(images) + 1), smem_spec(), vmem_spec()),
        scratch_shapes=product_scratch(points, halves) + list_scratch(),
        compiler_params=pltpu.CompilerParams(vmem_limit_bytes=15 * MIB),
        cost_estimate=light_cost(),
        name="eval_product",
    )(*operands)
    return tuple(out[: len(images)]), tuple(out[len(images) :])


def unsort_kernel(points, ranks, source, out):
    def gather(step, carry):
        at = pl.multiple_of(step * 8, 8)
        out[pl.ds(at, 8), :] = jnp.concatenate(
            [source[pl.ds(ranks[0, at + k], 1), :] for k in range(8)], axis=0
        )
        return carry

    lax.fori_loop(0, points // 8, gather, 0, unroll=4)


def unsort(ranks, source):
    points = ranks.shape[1]
    return pl.pallas_call(
        functools.partial(unsort_kernel, points),
        out_shape=jax.ShapeDtypeStruct((points, LANES), F32),
        in_specs=[smem_spec(), vmem_spec()],
        out_specs=vmem_spec(),
        compiler_params=pltpu.CompilerParams(vmem_limit_bytes=8 * MIB),
        cost_estimate=light_cost(),
        name="unsort",
    )(ranks, source)


def pair_swap(block):
    count = lax.axis_size("tm")
    return lax.ppermute(block, "tm", [(i, i ^ 1) for i in range(count)])


def pair_shift(block, turn=0):
    count = lax.axis_size("tm")
    route = []
    for i in range(count):
        source = i - 2 if i % 2 == turn else i + 2
        if 0 <= source < count:
            route.append((source, i))
    return lax.ppermute(block, "tm", route)


def core_swap(block):
    count = lax.axis_size("tile")
    return lax.ppermute(block, "tile", [(i, i ^ 1) for i in range(count)])


def after(value, *earlier):
    return lax.optimization_barrier((value, *earlier))[0]


def stride_sum(value, step):
    count = lax.axis_size("tm")
    return value + lax.ppermute(value, "tm", [(i, i ^ step) for i in range(count)])


def far_strides():
    step, steps = 2, []
    while step < lax.axis_size("tm"):
        steps.append(step)
        step *= 2
    return steps


def total(value, beside):
    value = value + core_swap(value)
    steps = [1] + far_strides()
    for step in steps[:-1]:
        value = stride_sum(value, step)
    return stride_sum(after(value, beside), steps[-1])


def local(coords, anomalies, noise_var):
    points = anomalies.shape[0]
    operands = [pltpu.with_memory_space_constraint(x, pltpu.HBM) for x in (coords, noise_var[None, :], anomalies)]
    given, whole, rows, ranks = sort_points(*operands)

    near = [pair_swap(c) for c in given]
    turned = pair_shift(given[1], 1)
    mates = core_swap(whole)
    image, own_eval = eval_product(points, given[0], rows, (given, (mates,)), OWN_SLOTS)
    near[0] = after(near[0], image[0], turned)
    far = [pair_shift(near[0])]
    far.append(pair_swap(after(turned, near[1], near[0])))
    near_mates = [core_swap(c) for c in near]
    image, near_eval = eval_product(points, given[0], rows, (near,), SLOTS, image)
    far = [after(far[0], image[0], far[1]), far[1]]
    far_mates = [core_swap(c) for c in far]
    image, far_eval = eval_product(points, given[0], rows, (far,), SLOTS, image)
    (*once, whole), mate_eval = eval_product(points, given[0], rows, (near_mates, far_mates), SLOTS, image, True)

    near = [pair_swap(c) for c in once]
    turned = pair_shift(once[-1], 1)
    mates = core_swap(whole)
    image0 = unsort(ranks, after(whole, mates))
    image = product(points, own_eval, rows, (once, (after(mates, image0),)))
    near[0] = after(near[0], image[0], turned)
    far = [pair_shift(c) for c in near[:-1]]
    far.append(pair_swap(after(turned, near[-1], near[0])))
    near_mates = [core_swap(c) for c in near]
    image = product(points, near_eval, rows, (near,), image)
    far_mates = [core_swap(after(c, image[0])) for c in far]
    image = product(points, far_eval, rows, (far,), image)
    twice, sums = product(points, mate_eval, rows, (near_mates, far_mates), image, False, all_sums, given, once)
    image1 = unsort(ranks, twice)

    sums = total(sums, image1)
    rr0, curve0, once_once, given_twice, once_twice = [sums[k : k + 1] for k in range(5)]
    alpha0 = rr0 / curve0
    rr1 = rr0 - 2.0 * alpha0 * curve0 + alpha0 * alpha0 * once_once
    beta = rr1 / rr0
    more = 1.0 + beta
    curve1 = more * more * curve0 - more * alpha0 * (given_twice + once_once) + alpha0 * alpha0 * once_twice
    alpha1 = rr1 / curve1
    residual = anomalies - alpha0 * image0
    weights = alpha0 * anomalies + alpha1 * (residual + beta * anomalies)
    again = (image0 - alpha0 * image1) + beta * image0
    return weights, residual - alpha1 * again


def solution(mesh):
    placed = (
        P(None, ("region", "tm", "tile")),
        P(("region", "tm", "tile"), None),
        P(("region", "tm", "tile")),
    )
    return jax.shard_map(
        local,
        mesh=mesh,
        in_specs=placed,
        out_specs=(P(("region", "tm", "tile"), None), P(("region", "tm", "tile"), None)),
        check_vma=False,
    )
```

```python
import functools

import jax
import jax.numpy as jnp
from jax import lax
from jax.experimental import pallas as pl
from jax.experimental.pallas import tpu as pltpu
from jax.sharding import PartitionSpec as P

LANES = 128
ROWS = 224
SLOTS = 40
UNROLL = 8
EVAL_UNROLL = 4
FIRST_CUTS = (0, 6, 12, 16)
LATER_CUTS = (0, 6, 12, 16)
FAR = 1.0e6
F32 = jnp.float32
BF16 = jnp.bfloat16
MIB = 1 << 20


def vmem_spec():
    return pl.BlockSpec(memory_space=pltpu.VMEM)


def smem_spec():
    return pl.BlockSpec(memory_space=pltpu.SMEM)


def split2(value):
    high = value.astype(BF16)
    low = (value - high.astype(F32)).astype(BF16)
    return high, low


def list_length(points, halves):
    return halves * (points // LANES) * -(-points // ROWS) + UNROLL


def header_rows(points):
    return -(-(3 * (points // LANES) + 3) // 8) * 8


def piece_sizes(points, cuts):
    rows = [points // LANES * cut // 16 * LANES for cut in cuts]
    return [b - a for a, b in zip(rows, rows[1:])]


def spans(chunks, top):
    found, start = [], 0
    for c, chunk in enumerate(chunks):
        skip = top if c == 0 else 0
        found.append((chunk, start, skip, chunk.shape[0] - skip))
        start += chunk.shape[0] - skip
    return found


def group_rows(chunks, top, start):
    for chunk, begin, skip, size in spans(chunks, top):
        if begin <= start < begin + size:
            return chunk, slice(start - begin + skip, start - begin + skip + LANES)
    raise ValueError(start)


def read_rows(chunks, top, start):
    chunk, here = group_rows(chunks, top, start)
    return chunk[here, :]


def sort_kernel(points, coords_hbm, noise_hbm, values_hbm, *refs):
    pieces = len(FIRST_CUTS) - 1
    out_values, refs = refs[: pieces + 1], refs[pieces + 1 :]
    rows, ranks, coords, noise, values, xcol, facts, sorted_facts, sorted_values, rank_row, rank_smem, sems = refs
    fetches = [
        pltpu.make_async_copy(source, target, sems.at[k])
        for k, (source, target) in enumerate(((coords_hbm, coords), (noise_hbm, noise), (values_hbm, values)))
    ]
    for fetch in fetches:
        fetch.start()
    fetches[0].wait()
    groups = points // LANES
    for g in range(groups):
        here = slice(g * LANES, (g + 1) * LANES)
        xcol[here, :] = jnp.transpose(jnp.broadcast_to(coords[1:2, here], (LANES, LANES)))

    xrow = [jnp.broadcast_to(coords[1:2, g * LANES : (g + 1) * LANES], (8, LANES)) for g in range(groups)]
    lane = lax.broadcasted_iota(jnp.int32, (8, LANES), 1)
    sub = lax.broadcasted_iota(jnp.int32, (8, LANES), 0)
    counts = tuple(jnp.zeros((8, LANES), F32) for _ in range(groups))
    for jg in range(groups):

        def count(step, carry):
            at = pl.multiple_of(jg * LANES + step * 8, 8)
            mine = xcol[pl.ds(at, 8), :]
            out = []
            for ig in range(groups):
                if ig == jg:
                    before = jnp.logical_or(
                        mine < xrow[ig],
                        jnp.logical_and(mine == xrow[ig], sub + step * 8 < lane),
                    )
                elif ig > jg:
                    before = mine <= xrow[ig]
                else:
                    before = mine < xrow[ig]
                out.append(carry[ig] + jnp.where(before, 1.0, 0.0))
            return tuple(out)

        counts = lax.fori_loop(0, LANES // 8, count, counts, unroll=2)
    for g in range(groups):
        rank_row[0:1, g * LANES : (g + 1) * LANES] = jnp.sum(counts[g], axis=0, keepdims=True).astype(jnp.int32)
    ranks[...] = rank_row[...]
    copy = pltpu.make_async_copy(rank_row, rank_smem, sems.at[3])
    copy.start()
    fetches[1].wait()
    blank = jnp.zeros((LANES - 4, LANES), F32)
    for g in range(groups):
        here = slice(g * LANES, (g + 1) * LANES)
        facts[here, :] = jnp.transpose(jnp.concatenate([coords[:, here], noise[:, here], blank], axis=0))
    copy.wait()
    fetches[2].wait()

    def scatter(step, carry):
        at = pl.multiple_of(step * 8, 8)
        block = values[pl.ds(at, 8), :]
        fact = facts[pl.ds(at, 8), :]
        for k in range(8):
            to = rank_smem[0, at + k]
            sorted_facts[pl.ds(to, 1), :] = fact[k : k + 1, :]
            sorted_values[pl.ds(to, 1), :] = block[k : k + 1, :]
        return carry

    lax.fori_loop(0, points // 8, scatter, 0, unroll=4)
    header = header_rows(points)
    whole = out_values[pieces]
    whole[header:, :] = sorted_values[...]
    for chunk, start, skip, size in spans(out_values[:pieces], header):
        chunk[skip:, :] = sorted_values[start : start + size, :]
    head = out_values[0]
    for g in range(groups):
        here = slice(g * LANES, (g + 1) * LANES)
        got = sorted_facts[here, :]
        flat = jnp.transpose(got)
        for k in range(4):
            if k < 3:
                head[k * groups + g : k * groups + g + 1, :] = flat[k : k + 1, :]
            scale = 4.0 if k < 3 else 1.0
            rows[k, here, :] = jnp.broadcast_to(got[:, k : k + 1] * scale, (LANES, LANES))
    for k in range(4):
        rows[k, points:, :] = jnp.full((ROWS, LANES), FAR if k < 3 else 0.0, F32)
    end = 3 * groups
    head[end : end + 1, :] = jnp.full((1, LANES), jnp.min(coords[0:1, :]), F32)
    head[end + 1 : end + 2, :] = jnp.full((1, LANES), jnp.max(coords[0:1, :]), F32)
    head[end + 2 : header, :] = jnp.ones((header - end - 2, LANES), F32)
    whole[0:header, :] = head[0:header, :]


def sort_points(coords, noise, values):
    points, width = values.shape
    header = header_rows(points)
    sizes = piece_sizes(points, FIRST_CUTS)
    out = pl.pallas_call(
        functools.partial(sort_kernel, points),
        out_shape=tuple(
            jax.ShapeDtypeStruct((size + (header if c in (0, len(sizes)) else 0), width), F32)
            for c, size in enumerate([*sizes, points])
        )
        + (
            pltpu.VMEM((4, points + ROWS, LANES), F32),
            jax.ShapeDtypeStruct((1, points), jnp.int32),
        ),
        in_specs=[pl.BlockSpec(memory_space=pltpu.HBM)] * 3,
        out_specs=[vmem_spec()] * (len(sizes) + 3),
        scratch_shapes=[
            pltpu.VMEM((3, points), F32),
            pltpu.VMEM((1, points), F32),
            pltpu.VMEM((points, width), F32),
            pltpu.VMEM((points, LANES), F32),
            pltpu.VMEM((points, LANES), F32),
            pltpu.VMEM((points, LANES), F32),
            pltpu.VMEM((points, LANES), F32),
            pltpu.VMEM((1, points), jnp.int32),
            pltpu.SMEM((1, points), jnp.int32),
            pltpu.SemaphoreType.DMA((4,)),
        ],
        compiler_params=pltpu.CompilerParams(vmem_limit_bytes=14 * MIB),
        name="sort_points",
    )(coords, noise, values)
    return out[: len(sizes)], *out[len(sizes) :]


def tile_values(rows, cols, at, count):
    span = pl.ds(at, count)
    dtime = jnp.abs(rows[0, span, :] - cols[0])
    dx = rows[1, span, :] - cols[1]
    dy = rows[2, span, :] - cols[2]
    square = jnp.maximum(dx * dx + dy * dy, 1e-30)
    dist = square * lax.rsqrt(square)
    near = jnp.maximum(4.0 - dtime, 0.0) * jnp.maximum(4.0 - dist, 0.0)
    near = near * near
    return near * near * ((dtime + 1.0) * (dist + 1.0))


def fill_tile(tile, rows, facts, w, step, at):
    cols = [jnp.broadcast_to(facts[pl.ds(k * step + w, 1), :], (16, LANES)) for k in range(3)]
    for part in range(ROWS // 16):
        start = pl.multiple_of(at + part * 16, 16)
        high, low = split2(tile_values(rows, cols, start, 16))
        tile[part * 16 : (part + 1) * 16, 0:LANES] = high
        tile[part * 16 : (part + 1) * 16, LANES:] = low


def gather_facts(windows, facts, heads):
    for half, head in enumerate(heads):
        for k in range(3):
            base = (len(heads) * k + half) * windows
            facts[base : base + windows, :] = head[k * windows : (k + 1) * windows, :] * 4.0


def find_ranges(points, own, other):
    windows = points // LANES
    early, late, mark = 3 * windows, 3 * windows + 1, 3 * windows + 2
    x = other[windows : 2 * windows, :]
    low = jnp.broadcast_to(x[:, 0:1], (windows, LANES))
    high = jnp.broadcast_to(x[:, LANES - 1 : LANES], (windows, LANES))
    begin = jnp.zeros((windows, LANES), F32)
    beyond = jnp.zeros((windows, LANES), F32)
    for g in range(windows):
        row = jnp.broadcast_to(own[windows + g : windows + g + 1, :], (windows, LANES))
        begin = begin + jnp.where(low - row >= 1.0, 1.0, 0.0)
        beyond = beyond + jnp.where(row - high >= 1.0, 1.0, 0.0)
    begin = jnp.sum(begin, axis=1, keepdims=True)
    end = points - jnp.sum(beyond, axis=1, keepdims=True)
    first = begin.astype(jnp.int32) // 16 * 16
    length = end - first.astype(F32)
    blocks = jnp.zeros((windows, 1), F32)
    for k in range(-(-points // ROWS)):
        blocks = blocks + jnp.where(length > float(k * ROWS), 1.0, 0.0)
    apart = jnp.maximum(
        other[early : early + 1, 0:1] - own[late : late + 1, 0:1],
        own[early : early + 1, 0:1] - other[late : late + 1, 0:1],
    )
    apart = jnp.where(other[mark : mark + 1, 0:1] > 0.5, apart, 2.0)
    blocks = jnp.where(jnp.logical_and(end > begin, jnp.broadcast_to(apart, (windows, 1)) < 1.0), blocks, 0.0)
    return jnp.broadcast_to(first * 64 + blocks.astype(jnp.int32), (windows, LANES))


def list_tiles(points, own, heads, work, facts, table, table_smem, sem, beside):
    windows = points // LANES
    found = jnp.concatenate([find_ranges(points, own, head) for head in heads], axis=0)
    lane = lax.broadcasted_iota(jnp.int32, found.shape, 1)
    sub = lax.broadcasted_iota(jnp.int32, found.shape, 0)
    table[...] = jnp.sum(jnp.where(lane == sub, found, 0), axis=0, keepdims=True)
    copy = pltpu.make_async_copy(table, table_smem, sem)
    copy.start()
    gather_facts(windows, facts, heads)
    beside()
    copy.wait()
    slot = jnp.int32(0)
    for w in range(len(heads) * windows):
        packed = table_smem[0, w]
        first = lax.shift_right_logical(packed, 6)
        blocks = lax.bitwise_and(packed, 63)
        for b in range(2):
            work[0, slot + b] = first + b * ROWS
            work[1, slot + b] = w

        @pl.when(blocks > 2)
        def _(slot=slot, first=first, blocks=blocks, w=w):
            def block(b, carry):
                work[0, slot + b] = first + b * ROWS
                work[1, slot + b] = w
                return carry

            lax.fori_loop(2, blocks, block, 0)

        slot = slot + blocks
    for k in range(UNROLL):
        work[0, slot + k] = points
        work[1, slot + k] = 0
    work[2, 0] = slot
    return slot


def keep_tiles(windows, work, facts, rows, cache, step):
    for k in range(EVAL_UNROLL):
        s = step * EVAL_UNROLL + k
        fill_tile(cache.at[s], rows, facts, work[1, s], windows, pl.multiple_of(work[0, s], 16))


def kept_shapes(points, halves):
    return (
        pltpu.VMEM((SLOTS, ROWS, 2 * LANES), BF16),
        jax.ShapeDtypeStruct((3, list_length(points, halves)), jnp.int32),
        jax.ShapeDtypeStruct((3 * halves * (points // LANES), LANES), F32),
    )


def list_scratch():
    return [pltpu.VMEM((1, LANES), jnp.int32), pltpu.SMEM((1, LANES), jnp.int32), pltpu.SemaphoreType.DMA]


def light_cost():
    return pl.CostEstimate(flops=1_000_000, bytes_accessed=100_000, transcendentals=0)


def split_values(points, values, top, pairs):
    for half, chunks in enumerate(values):
        for chunk, start, skip, size in spans(chunks, top):
            base = half * (points // LANES) + start // LANES

            def split(w, carry):
                high, low = split2(chunk[pl.ds(pl.multiple_of(skip + w * LANES, 8), LANES), :])
                both = jnp.concatenate([high, low], axis=1)
                pairs[base + w, 0:LANES, :] = both
                pairs[base + w, LANES:, :] = both
                return carry

            lax.fori_loop(0, size // LANES, split, 0)


def multiply(work, cache, pairs, acc, step, count):
    for k in range(count):
        s = step * count + k
        at = pl.multiple_of(work[0, s], 16)
        acc[pl.ds(at, ROWS), :] += jnp.dot(cache[s], pairs[work[1, s]], preferred_element_type=F32)


def multiply_rest(windows, work, facts, rows, cache, pairs, acc, tile, total):
    slots = cache.shape[0]

    @pl.when(total > slots)
    def _():
        def again(s, carry):
            at = pl.multiple_of(work[0, s], 16)
            w = work[1, s]
            fill_tile(tile, rows, facts, w, windows, at)
            acc[pl.ds(at, ROWS), :] += jnp.dot(tile[...], pairs[w], preferred_element_type=F32)
            return carry

        lax.fori_loop(slots, total, again, 0)


def finish(points, header, top, marker, rows, acc, groups):
    first, (before, given, once, out, sums) = groups[0], groups[-5:]
    marks = [jnp.zeros((8, LANES), F32)] * 5
    for start in range(0, points, LANES):
        here = slice(start, start + LANES)
        image = (acc[here, 0:LANES] + acc[here, LANES:]) * (2.0**-16)
        if before:
            image = image + read_rows(before, 0, start)
        else:
            image = image + rows[3, here, :] * read_rows(first, top, start)
        if len(out) > 1:
            target, place = group_rows(out[:-1], 0, start)
            target[place, :] = image
        out[-1][here, :] = image
        if marker is not None:
            marks = marker(marks, image, read_rows(given, header, start), read_rows(once, 0, start))
    if marker is not None:
        sums[0][...] = jnp.zeros((8, LANES), F32)
        for k in range(5):
            sums[0][k : k + 1, :] = jnp.sum(marks[k], axis=0, keepdims=True)


def take_groups(refs, counts):
    groups = []
    for count in counts:
        groups.append(refs[:count])
        refs = refs[count:]
    return groups, refs


def product_kernel(points, halves, headed, counts, marker, work, facts, rows, cache, *refs):
    groups, (acc, pairs, tile) = take_groups(refs, counts)
    header = header_rows(points)
    top = header if headed else 0
    total = work[2, 0]
    acc[...] = jnp.zeros_like(acc)

    @pl.when(total > 0)
    def _():
        split_values(points, groups[:halves], top, pairs)

        def slots(step, carry):
            multiply(work, cache, pairs, acc, step, UNROLL)
            return carry

        kept = jnp.minimum(total, cache.shape[0])
        lax.fori_loop(0, (kept + (UNROLL - 1)) // UNROLL, slots, 0)
        multiply_rest(halves * (points // LANES), work, facts, rows, cache, pairs, acc, tile, total)

    finish(points, header, top, marker, rows, acc, groups)


def both_kernel(points, halves, counts, own, rows, *refs):
    windows = halves * (points // LANES)
    groups, refs = take_groups(refs, counts)
    values = groups[:halves]
    cache, work, facts, acc, pairs, tile, table, table_smem, sem = refs
    header = header_rows(points)

    def prepare():
        acc[...] = jnp.zeros_like(acc)
        split_values(points, values, header, pairs)

    heads = [half[0] for half in values]
    total = list_tiles(points, own, heads, work, facts, table, table_smem, sem, prepare)

    @pl.when(total > 0)
    def _():
        kept = jnp.minimum(total, cache.shape[0])
        steps = (kept + (EVAL_UNROLL - 1)) // EVAL_UNROLL
        keep_tiles(windows, work, facts, rows, cache, 0)

        def slots(step, carry):
            multiply(work, cache, pairs, acc, step - 1, EVAL_UNROLL)
            keep_tiles(windows, work, facts, rows, cache, step)
            return carry

        lax.fori_loop(1, steps, slots, 0)
        multiply(work, cache, pairs, acc, steps - 1, EVAL_UNROLL)
        multiply_rest(windows, work, facts, rows, cache, pairs, acc, tile, total)

    finish(points, header, header, None, rows, acc, groups)


def product_scratch(points, halves):
    return [
        pltpu.VMEM((points + ROWS, 2 * LANES), F32),
        pltpu.VMEM((halves * (points // LANES), 2 * LANES, 2 * LANES), BF16),
        pltpu.VMEM((ROWS, 2 * LANES), BF16),
    ]


def image_shapes(points, sent):
    sizes = [*(piece_sizes(points, LATER_CUTS) if sent else []), points]
    return [jax.ShapeDtypeStruct((size, LANES), F32) for size in sizes]


def fold(value):
    return jnp.sum(value.reshape(value.shape[0] // 8, 8, LANES), axis=0)


def all_sums(marks, image, given, once):
    terms = (given * given, given * once, once * once, given * image, once * image)
    return [mark + fold(term) for mark, term in zip(marks, terms)]


def product(points, evaluated, rows, values, before=(), headed=False, marker=None, given=(), once=()):
    cache, work, facts = evaluated
    groups = (*values, before, given, once)
    operands = (facts, rows, cache, *(x for group in groups for x in group))
    sums = int(marker is not None)
    counts = [len(group) for group in groups] + [1, sums]
    out = pl.pallas_call(
        functools.partial(product_kernel, points, len(values), headed, counts, marker),
        out_shape=image_shapes(points, False) + [jax.ShapeDtypeStruct((8, LANES), F32)] * sums,
        in_specs=[smem_spec()] + [vmem_spec()] * len(operands),
        out_specs=[vmem_spec()] * (1 + sums),
        scratch_shapes=product_scratch(points, len(values)),
        compiler_params=pltpu.CompilerParams(vmem_limit_bytes=15 * MIB),
        cost_estimate=light_cost(),
        name="product",
    )(work, *operands)
    return tuple(out)


def eval_product(points, own, rows, values, before=(), sent=False):
    halves = len(values)
    groups = (*values, before, (), ())
    operands = (own, rows, *(x for group in groups for x in group))
    images = image_shapes(points, sent)
    counts = [len(group) for group in groups] + [len(images), 0]
    out = pl.pallas_call(
        functools.partial(both_kernel, points, halves, counts),
        out_shape=(*images, *kept_shapes(points, halves)),
        in_specs=[vmem_spec()] * len(operands),
        out_specs=(*[vmem_spec()] * (len(images) + 1), smem_spec(), vmem_spec()),
        scratch_shapes=product_scratch(points, halves) + list_scratch(),
        compiler_params=pltpu.CompilerParams(vmem_limit_bytes=15 * MIB),
        cost_estimate=light_cost(),
        name="eval_product",
    )(*operands)
    return tuple(out[: len(images)]), tuple(out[len(images) :])


def unsort_kernel(points, ranks, source, out):
    def gather(step, carry):
        at = pl.multiple_of(step * 8, 8)
        out[pl.ds(at, 8), :] = jnp.concatenate(
            [source[pl.ds(ranks[0, at + k], 1), :] for k in range(8)], axis=0
        )
        return carry

    lax.fori_loop(0, points // 8, gather, 0, unroll=4)


def unsort(ranks, source):
    points = ranks.shape[1]
    return pl.pallas_call(
        functools.partial(unsort_kernel, points),
        out_shape=jax.ShapeDtypeStruct((points, LANES), F32),
        in_specs=[smem_spec(), vmem_spec()],
        out_specs=vmem_spec(),
        compiler_params=pltpu.CompilerParams(vmem_limit_bytes=8 * MIB),
        cost_estimate=light_cost(),
        name="unsort",
    )(ranks, source)


def pair_swap(block):
    count = lax.axis_size("tm")
    return lax.ppermute(block, "tm", [(i, i ^ 1) for i in range(count)])


def pair_shift(block, turn=0):
    count = lax.axis_size("tm")
    route = []
    for i in range(count):
        source = i - 2 if i % 2 == turn else i + 2
        if 0 <= source < count:
            route.append((source, i))
    return lax.ppermute(block, "tm", route)


def core_swap(block):
    count = lax.axis_size("tile")
    return lax.ppermute(block, "tile", [(i, i ^ 1) for i in range(count)])


def after(value, *earlier):
    return lax.optimization_barrier((value, *earlier))[0]


def stride_sum(value, step):
    count = lax.axis_size("tm")
    return value + lax.ppermute(value, "tm", [(i, i ^ step) for i in range(count)])


def far_strides():
    step, steps = 2, []
    while step < lax.axis_size("tm"):
        steps.append(step)
        step *= 2
    return steps


def total(value, beside):
    value = value + core_swap(value)
    steps = [1] + far_strides()
    for step in steps[:-1]:
        value = stride_sum(value, step)
    return stride_sum(after(value, beside), steps[-1])


def local(coords, anomalies, noise_var):
    points = anomalies.shape[0]
    operands = [pltpu.with_memory_space_constraint(x, pltpu.HBM) for x in (coords, noise_var[None, :], anomalies)]
    given, whole, rows, ranks = sort_points(*operands)

    near = [pair_swap(c) for c in given]
    turned = pair_shift(given[-1], 1)
    mates = core_swap(whole)
    image, own_eval = eval_product(points, given[0], rows, (given,))
    near[0] = after(near[0], image[0], turned)
    far = [pair_shift(near[0])]
    image, mate_eval = eval_product(points, given[0], rows, ((after(mates, near[0]),),), image)
    near[1] = after(near[1], image[0])
    far.append(pair_shift(near[1]))
    far.append(pair_swap(after(turned, near[2], near[1])))
    near_mates = [core_swap(c) for c in near]
    image, near_eval = eval_product(points, given[0], rows, (near,), image)
    far = [after(c, image[0]) for c in far]
    far_mates = [core_swap(c) for c in far]
    image, far_eval = eval_product(points, given[0], rows, (far,), image)
    (*once, whole), rest_eval = eval_product(points, given[0], rows, (near_mates, far_mates), image, True)

    near = [pair_swap(c) for c in once]
    turned = pair_shift(once[-1], 1)
    mates = core_swap(whole)
    image0 = unsort(ranks, after(whole, mates))
    image = product(points, own_eval, rows, (once,))
    image = product(points, mate_eval, rows, ((after(mates, image0),),), image)
    near[0] = after(near[0], image[0], turned)
    far = [pair_shift(c) for c in near[:-1]]
    far.append(pair_swap(after(turned, near[-1], near[0])))
    near_mates = [core_swap(c) for c in near]
    image = product(points, near_eval, rows, (near,), image)
    far_mates = [core_swap(after(far[0], image[0])), core_swap(far[1]), core_swap(after(far[2], image[0]))]
    image = product(points, far_eval, rows, (far,), image)
    twice, sums = product(points, rest_eval, rows, (near_mates, far_mates), image, False, all_sums, given, once)
    image1 = unsort(ranks, twice)

    sums = total(sums, image1)
    rr0, curve0, once_once, given_twice, once_twice = [sums[k : k + 1] for k in range(5)]
    alpha0 = rr0 / curve0
    rr1 = rr0 - 2.0 * alpha0 * curve0 + alpha0 * alpha0 * once_once
    beta = rr1 / rr0
    more = 1.0 + beta
    curve1 = more * more * curve0 - more * alpha0 * (given_twice + once_once) + alpha0 * alpha0 * once_twice
    alpha1 = rr1 / curve1
    residual = anomalies - alpha0 * image0
    weights = alpha0 * anomalies + alpha1 * (residual + beta * anomalies)
    again = (image0 - alpha0 * image1) + beta * image0
    return weights, residual - alpha1 * again


def solution(mesh):
    placed = (
        P(None, ("region", "tm", "tile")),
        P(("region", "tm", "tile"), None),
        P(("region", "tm", "tile")),
    )
    return jax.shard_map(
        local,
        mesh=mesh,
        in_specs=placed,
        out_specs=(P(("region", "tm", "tile"), None), P(("region", "tm", "tile"), None)),
        check_vma=False,
    )
```

```python
import functools

import jax
import jax.numpy as jnp
from jax import lax
from jax.experimental import pallas as pl
from jax.experimental.pallas import tpu as pltpu
from jax.sharding import PartitionSpec as P

LANES = 128
ROWS = 224
SLOTS = 40
UNROLL = 8
EVAL_UNROLL = 4
FIRST_CUTS = (0, 6, 12, 16)
LATER_CUTS = (0, 6, 12, 16)
FAR = 1.0e6
F32 = jnp.float32
BF16 = jnp.bfloat16
MIB = 1 << 20


def vmem_spec():
    return pl.BlockSpec(memory_space=pltpu.VMEM)


def smem_spec():
    return pl.BlockSpec(memory_space=pltpu.SMEM)


def split2(value):
    high = value.astype(BF16)
    low = (value - high.astype(F32)).astype(BF16)
    return high, low


def list_length(points, halves):
    return halves * (points // LANES) * -(-points // ROWS) + UNROLL


def header_rows(points):
    return -(-(3 * (points // LANES) + 3) // 8) * 8


def piece_sizes(points, cuts):
    rows = [points // LANES * cut // 16 * LANES for cut in cuts]
    return [b - a for a, b in zip(rows, rows[1:])]


def spans(chunks, top):
    found, start = [], 0
    for c, chunk in enumerate(chunks):
        skip = top if c == 0 else 0
        found.append((chunk, start, skip, chunk.shape[0] - skip))
        start += chunk.shape[0] - skip
    return found


def group_rows(chunks, top, start):
    for chunk, begin, skip, size in spans(chunks, top):
        if begin <= start < begin + size:
            return chunk, slice(start - begin + skip, start - begin + skip + LANES)
    raise ValueError(start)


def read_rows(chunks, top, start):
    chunk, here = group_rows(chunks, top, start)
    return chunk[here, :]


def sort_kernel(points, coords_hbm, noise_hbm, values_hbm, *refs):
    pieces = len(FIRST_CUTS) - 1
    out_values, refs = refs[: pieces + 1], refs[pieces + 1 :]
    rows, ranks, coords, noise, values, xcol, facts, sorted_facts, sorted_values, rank_row, rank_smem, sems = refs
    fetches = [
        pltpu.make_async_copy(source, target, sems.at[k])
        for k, (source, target) in enumerate(((coords_hbm, coords), (noise_hbm, noise), (values_hbm, values)))
    ]
    for fetch in fetches:
        fetch.start()
    fetches[0].wait()
    groups = points // LANES
    for g in range(groups):
        here = slice(g * LANES, (g + 1) * LANES)
        xcol[here, :] = jnp.transpose(jnp.broadcast_to(coords[1:2, here], (LANES, LANES)))

    xrow = [jnp.broadcast_to(coords[1:2, g * LANES : (g + 1) * LANES], (8, LANES)) for g in range(groups)]
    lane = lax.broadcasted_iota(jnp.int32, (8, LANES), 1)
    sub = lax.broadcasted_iota(jnp.int32, (8, LANES), 0)
    counts = tuple(jnp.zeros((8, LANES), F32) for _ in range(groups))
    for jg in range(groups):

        def count(step, carry):
            at = pl.multiple_of(jg * LANES + step * 8, 8)
            mine = xcol[pl.ds(at, 8), :]
            out = []
            for ig in range(groups):
                if ig == jg:
                    before = jnp.logical_or(
                        mine < xrow[ig],
                        jnp.logical_and(mine == xrow[ig], sub + step * 8 < lane),
                    )
                elif ig > jg:
                    before = mine <= xrow[ig]
                else:
                    before = mine < xrow[ig]
                out.append(carry[ig] + jnp.where(before, 1.0, 0.0))
            return tuple(out)

        counts = lax.fori_loop(0, LANES // 8, count, counts, unroll=4)
    for g in range(groups):
        rank_row[0:1, g * LANES : (g + 1) * LANES] = jnp.sum(counts[g], axis=0, keepdims=True).astype(jnp.int32)
    ranks[...] = rank_row[...]
    copy = pltpu.make_async_copy(rank_row, rank_smem, sems.at[3])
    copy.start()
    fetches[1].wait()
    blank = jnp.zeros((LANES - 4, LANES), F32)
    for g in range(groups):
        here = slice(g * LANES, (g + 1) * LANES)
        facts[here, :] = jnp.transpose(jnp.concatenate([coords[:, here], noise[:, here], blank], axis=0))
    copy.wait()
    fetches[2].wait()

    def scatter(step, carry):
        at = pl.multiple_of(step * 8, 8)
        block = values[pl.ds(at, 8), :]
        fact = facts[pl.ds(at, 8), :]
        for k in range(8):
            to = rank_smem[0, at + k]
            sorted_facts[pl.ds(to, 1), :] = fact[k : k + 1, :]
            sorted_values[pl.ds(to, 1), :] = block[k : k + 1, :]
        return carry

    lax.fori_loop(0, points // 8, scatter, 0, unroll=8)
    header = header_rows(points)
    whole = out_values[pieces]
    whole[header:, :] = sorted_values[...]
    for chunk, start, skip, size in spans(out_values[:pieces], header):
        chunk[skip:, :] = sorted_values[start : start + size, :]
    head = out_values[0]
    for g in range(groups):
        here = slice(g * LANES, (g + 1) * LANES)
        got = sorted_facts[here, :]
        flat = jnp.transpose(got)
        for k in range(4):
            if k < 3:
                head[k * groups + g : k * groups + g + 1, :] = flat[k : k + 1, :]
            scale = 4.0 if k < 3 else 1.0
            rows[k, here, :] = jnp.broadcast_to(got[:, k : k + 1] * scale, (LANES, LANES))
    for k in range(4):
        rows[k, points:, :] = jnp.full((ROWS, LANES), FAR if k < 3 else 0.0, F32)
    end = 3 * groups
    head[end : end + 1, :] = jnp.full((1, LANES), jnp.min(coords[0:1, :]), F32)
    head[end + 1 : end + 2, :] = jnp.full((1, LANES), jnp.max(coords[0:1, :]), F32)
    head[end + 2 : header, :] = jnp.ones((header - end - 2, LANES), F32)
    whole[0:header, :] = head[0:header, :]


def sort_points(coords, noise, values):
    points, width = values.shape
    header = header_rows(points)
    sizes = piece_sizes(points, FIRST_CUTS)
    out = pl.pallas_call(
        functools.partial(sort_kernel, points),
        out_shape=tuple(
            jax.ShapeDtypeStruct((size + (header if c in (0, len(sizes)) else 0), width), F32)
            for c, size in enumerate([*sizes, points])
        )
        + (
            pltpu.VMEM((4, points + ROWS, LANES), F32),
            jax.ShapeDtypeStruct((1, points), jnp.int32),
        ),
        in_specs=[pl.BlockSpec(memory_space=pltpu.HBM)] * 3,
        out_specs=[vmem_spec()] * (len(sizes) + 3),
        scratch_shapes=[
            pltpu.VMEM((3, points), F32),
            pltpu.VMEM((1, points), F32),
            pltpu.VMEM((points, width), F32),
            pltpu.VMEM((points, LANES), F32),
            pltpu.VMEM((points, LANES), F32),
            pltpu.VMEM((points, LANES), F32),
            pltpu.VMEM((points, LANES), F32),
            pltpu.VMEM((1, points), jnp.int32),
            pltpu.SMEM((1, points), jnp.int32),
            pltpu.SemaphoreType.DMA((4,)),
        ],
        compiler_params=pltpu.CompilerParams(vmem_limit_bytes=14 * MIB),
        name="sort_points",
    )(coords, noise, values)
    return out[: len(sizes)], *out[len(sizes) :]


def tile_values(rows, cols, at, count):
    span = pl.ds(at, count)
    dtime = jnp.abs(rows[0, span, :] - cols[0])
    dx = rows[1, span, :] - cols[1]
    dy = rows[2, span, :] - cols[2]
    square = jnp.maximum(dx * dx + dy * dy, 1e-30)
    dist = square * lax.rsqrt(square)
    near = jnp.maximum(4.0 - dtime, 0.0) * jnp.maximum(4.0 - dist, 0.0)
    near = near * near
    return near * near * ((dtime + 1.0) * (dist + 1.0))


def fill_tile(tile, rows, facts, w, step, at):
    cols = [jnp.broadcast_to(facts[pl.ds(k * step + w, 1), :], (16, LANES)) for k in range(3)]
    for part in range(ROWS // 16):
        start = pl.multiple_of(at + part * 16, 16)
        high, low = split2(tile_values(rows, cols, start, 16))
        tile[part * 16 : (part + 1) * 16, 0:LANES] = high
        tile[part * 16 : (part + 1) * 16, LANES:] = low


def gather_facts(windows, facts, heads):
    for half, head in enumerate(heads):
        for k in range(3):
            base = (len(heads) * k + half) * windows
            facts[base : base + windows, :] = head[k * windows : (k + 1) * windows, :] * 4.0


def find_ranges(points, own, other):
    windows = points // LANES
    early, late, mark = 3 * windows, 3 * windows + 1, 3 * windows + 2
    x = other[windows : 2 * windows, :]
    low = jnp.broadcast_to(x[:, 0:1], (windows, LANES))
    high = jnp.broadcast_to(x[:, LANES - 1 : LANES], (windows, LANES))
    begin = jnp.zeros((windows, LANES), F32)
    beyond = jnp.zeros((windows, LANES), F32)
    for g in range(windows):
        row = jnp.broadcast_to(own[windows + g : windows + g + 1, :], (windows, LANES))
        begin = begin + jnp.where(low - row >= 1.0, 1.0, 0.0)
        beyond = beyond + jnp.where(row - high >= 1.0, 1.0, 0.0)
    begin = jnp.sum(begin, axis=1, keepdims=True)
    end = points - jnp.sum(beyond, axis=1, keepdims=True)
    first = begin.astype(jnp.int32) // 16 * 16
    length = end - first.astype(F32)
    blocks = jnp.zeros((windows, 1), F32)
    for k in range(-(-points // ROWS)):
        blocks = blocks + jnp.where(length > float(k * ROWS), 1.0, 0.0)
    apart = jnp.maximum(
        other[early : early + 1, 0:1] - own[late : late + 1, 0:1],
        own[early : early + 1, 0:1] - other[late : late + 1, 0:1],
    )
    apart = jnp.where(other[mark : mark + 1, 0:1] > 0.5, apart, 2.0)
    blocks = jnp.where(jnp.logical_and(end > begin, jnp.broadcast_to(apart, (windows, 1)) < 1.0), blocks, 0.0)
    return jnp.broadcast_to(first * 64 + blocks.astype(jnp.int32), (windows, LANES))


def list_tiles(points, own, heads, work, facts, table, table_smem, sem, beside):
    windows = points // LANES
    found = jnp.concatenate([find_ranges(points, own, head) for head in heads], axis=0)
    lane = lax.broadcasted_iota(jnp.int32, found.shape, 1)
    sub = lax.broadcasted_iota(jnp.int32, found.shape, 0)
    table[...] = jnp.sum(jnp.where(lane == sub, found, 0), axis=0, keepdims=True)
    copy = pltpu.make_async_copy(table, table_smem, sem)
    copy.start()
    gather_facts(windows, facts, heads)
    beside()
    copy.wait()
    slot = jnp.int32(0)
    for w in range(len(heads) * windows):
        packed = table_smem[0, w]
        first = lax.shift_right_logical(packed, 6)
        blocks = lax.bitwise_and(packed, 63)
        for b in range(2):
            work[0, slot + b] = first + b * ROWS
            work[1, slot + b] = w

        @pl.when(blocks > 2)
        def _(slot=slot, first=first, blocks=blocks, w=w):
            def block(b, carry):
                work[0, slot + b] = first + b * ROWS
                work[1, slot + b] = w
                return carry

            lax.fori_loop(2, blocks, block, 0)

        slot = slot + blocks
    for k in range(UNROLL):
        work[0, slot + k] = points
        work[1, slot + k] = 0
    work[2, 0] = slot
    return slot


def keep_tiles(windows, work, facts, rows, cache, step):
    for k in range(EVAL_UNROLL):
        s = step * EVAL_UNROLL + k
        fill_tile(cache.at[s], rows, facts, work[1, s], windows, pl.multiple_of(work[0, s], 16))


def kept_shapes(points, halves):
    return (
        pltpu.VMEM((SLOTS, ROWS, 2 * LANES), BF16),
        jax.ShapeDtypeStruct((3, list_length(points, halves)), jnp.int32),
        jax.ShapeDtypeStruct((3 * halves * (points // LANES), LANES), F32),
    )


def list_scratch():
    return [pltpu.VMEM((1, LANES), jnp.int32), pltpu.SMEM((1, LANES), jnp.int32), pltpu.SemaphoreType.DMA]


def light_cost():
    return pl.CostEstimate(flops=1_000_000, bytes_accessed=100_000, transcendentals=0)


def split_values(points, values, top, pairs):
    for half, chunks in enumerate(values):
        for chunk, start, skip, size in spans(chunks, top):
            base = half * (points // LANES) + start // LANES

            def split(w, carry):
                high, low = split2(chunk[pl.ds(pl.multiple_of(skip + w * LANES, 8), LANES), :])
                both = jnp.concatenate([high, low], axis=1)
                pairs[base + w, 0:LANES, :] = both
                pairs[base + w, LANES:, :] = both
                return carry

            lax.fori_loop(0, size // LANES, split, 0, unroll=2)


def multiply(work, cache, pairs, acc, step, count):
    for k in range(count):
        s = step * count + k
        at = pl.multiple_of(work[0, s], 16)
        acc[pl.ds(at, ROWS), :] += jnp.dot(cache[s], pairs[work[1, s]], preferred_element_type=F32)


def multiply_rest(windows, work, facts, rows, cache, pairs, acc, tile, total):
    slots = cache.shape[0]

    @pl.when(total > slots)
    def _():
        def again(s, carry):
            at = pl.multiple_of(work[0, s], 16)
            w = work[1, s]
            fill_tile(tile, rows, facts, w, windows, at)
            acc[pl.ds(at, ROWS), :] += jnp.dot(tile[...], pairs[w], preferred_element_type=F32)
            return carry

        lax.fori_loop(slots, total, again, 0)


def finish(points, header, top, marker, rows, acc, groups):
    first, (before, given, once, out, sums) = groups[0], groups[-5:]
    marks = [jnp.zeros((8, LANES), F32)] * 5
    for start in range(0, points, LANES):
        here = slice(start, start + LANES)
        image = (acc[here, 0:LANES] + acc[here, LANES:]) * (2.0**-16)
        if before:
            image = image + read_rows(before, 0, start)
        else:
            image = image + rows[3, here, :] * read_rows(first, top, start)
        if len(out) > 1:
            target, place = group_rows(out[:-1], 0, start)
            target[place, :] = image
        out[-1][here, :] = image
        if marker is not None:
            marks = marker(marks, image, read_rows(given, header, start), read_rows(once, 0, start))
    if marker is not None:
        sums[0][...] = jnp.zeros((8, LANES), F32)
        for k in range(5):
            sums[0][k : k + 1, :] = jnp.sum(marks[k], axis=0, keepdims=True)


def take_groups(refs, counts):
    groups = []
    for count in counts:
        groups.append(refs[:count])
        refs = refs[count:]
    return groups, refs


def product_kernel(points, halves, headed, counts, marker, work, facts, rows, cache, *refs):
    groups, (acc, pairs, tile) = take_groups(refs, counts)
    header = header_rows(points)
    top = header if headed else 0
    total = work[2, 0]
    acc[...] = jnp.zeros_like(acc)

    @pl.when(total > 0)
    def _():
        split_values(points, groups[:halves], top, pairs)

        def slots(step, carry):
            multiply(work, cache, pairs, acc, step, UNROLL)
            return carry

        kept = jnp.minimum(total, cache.shape[0])
        lax.fori_loop(0, (kept + (UNROLL - 1)) // UNROLL, slots, 0)
        multiply_rest(halves * (points // LANES), work, facts, rows, cache, pairs, acc, tile, total)

    finish(points, header, top, marker, rows, acc, groups)


def both_kernel(points, halves, counts, own, rows, *refs):
    windows = halves * (points // LANES)
    groups, refs = take_groups(refs, counts)
    values = groups[:halves]
    cache, work, facts, acc, pairs, tile, table, table_smem, sem = refs
    header = header_rows(points)

    def prepare():
        acc[...] = jnp.zeros_like(acc)
        split_values(points, values, header, pairs)

    heads = [half[0] for half in values]
    total = list_tiles(points, own, heads, work, facts, table, table_smem, sem, prepare)

    @pl.when(total > 0)
    def _():
        kept = jnp.minimum(total, cache.shape[0])
        steps = (kept + (EVAL_UNROLL - 1)) // EVAL_UNROLL
        keep_tiles(windows, work, facts, rows, cache, 0)

        def slots(step, carry):
            multiply(work, cache, pairs, acc, step - 1, EVAL_UNROLL)
            keep_tiles(windows, work, facts, rows, cache, step)
            return carry

        lax.fori_loop(1, steps, slots, 0)
        multiply(work, cache, pairs, acc, steps - 1, EVAL_UNROLL)
        multiply_rest(windows, work, facts, rows, cache, pairs, acc, tile, total)

    finish(points, header, header, None, rows, acc, groups)


def product_scratch(points, halves):
    return [
        pltpu.VMEM((points + ROWS, 2 * LANES), F32),
        pltpu.VMEM((halves * (points // LANES), 2 * LANES, 2 * LANES), BF16),
        pltpu.VMEM((ROWS, 2 * LANES), BF16),
    ]


def image_shapes(points, sent):
    sizes = [*(piece_sizes(points, LATER_CUTS) if sent else []), points]
    return [jax.ShapeDtypeStruct((size, LANES), F32) for size in sizes]


def fold(value):
    return jnp.sum(value.reshape(value.shape[0] // 8, 8, LANES), axis=0)


def all_sums(marks, image, given, once):
    terms = (given * given, given * once, once * once, given * image, once * image)
    return [mark + fold(term) for mark, term in zip(marks, terms)]


def product(points, evaluated, rows, values, before=(), headed=False, marker=None, given=(), once=()):
    cache, work, facts = evaluated
    groups = (*values, before, given, once)
    operands = (facts, rows, cache, *(x for group in groups for x in group))
    sums = int(marker is not None)
    counts = [len(group) for group in groups] + [1, sums]
    out = pl.pallas_call(
        functools.partial(product_kernel, points, len(values), headed, counts, marker),
        out_shape=image_shapes(points, False) + [jax.ShapeDtypeStruct((8, LANES), F32)] * sums,
        in_specs=[smem_spec()] + [vmem_spec()] * len(operands),
        out_specs=[vmem_spec()] * (1 + sums),
        scratch_shapes=product_scratch(points, len(values)),
        compiler_params=pltpu.CompilerParams(vmem_limit_bytes=15 * MIB),
        cost_estimate=light_cost(),
        name="product",
    )(work, *operands)
    return tuple(out)


def eval_product(points, own, rows, values, before=(), sent=False):
    halves = len(values)
    groups = (*values, before, (), ())
    operands = (own, rows, *(x for group in groups for x in group))
    images = image_shapes(points, sent)
    counts = [len(group) for group in groups] + [len(images), 0]
    out = pl.pallas_call(
        functools.partial(both_kernel, points, halves, counts),
        out_shape=(*images, *kept_shapes(points, halves)),
        in_specs=[vmem_spec()] * len(operands),
        out_specs=(*[vmem_spec()] * (len(images) + 1), smem_spec(), vmem_spec()),
        scratch_shapes=product_scratch(points, halves) + list_scratch(),
        compiler_params=pltpu.CompilerParams(vmem_limit_bytes=15 * MIB),
        cost_estimate=light_cost(),
        name="eval_product",
    )(*operands)
    return tuple(out[: len(images)]), tuple(out[len(images) :])


def unsort_kernel(points, ranks, source, out):
    def gather(step, carry):
        at = pl.multiple_of(step * 8, 8)
        out[pl.ds(at, 8), :] = jnp.concatenate(
            [source[pl.ds(ranks[0, at + k], 1), :] for k in range(8)], axis=0
        )
        return carry

    lax.fori_loop(0, points // 8, gather, 0, unroll=8)


def unsort(ranks, source):
    points = ranks.shape[1]
    return pl.pallas_call(
        functools.partial(unsort_kernel, points),
        out_shape=jax.ShapeDtypeStruct((points, LANES), F32),
        in_specs=[smem_spec(), vmem_spec()],
        out_specs=vmem_spec(),
        compiler_params=pltpu.CompilerParams(vmem_limit_bytes=8 * MIB),
        cost_estimate=light_cost(),
        name="unsort",
    )(ranks, source)


def pair_swap(block):
    count = lax.axis_size("tm")
    return lax.ppermute(block, "tm", [(i, i ^ 1) for i in range(count)])


def pair_shift(block, turn=0):
    count = lax.axis_size("tm")
    route = []
    for i in range(count):
        source = i - 2 if i % 2 == turn else i + 2
        if 0 <= source < count:
            route.append((source, i))
    return lax.ppermute(block, "tm", route)


def core_swap(block):
    count = lax.axis_size("tile")
    return lax.ppermute(block, "tile", [(i, i ^ 1) for i in range(count)])


def after(value, *earlier):
    return lax.optimization_barrier((value, *earlier))[0]


def stride_sum(value, step):
    count = lax.axis_size("tm")
    return value + lax.ppermute(value, "tm", [(i, i ^ step) for i in range(count)])


def far_strides():
    step, steps = 2, []
    while step < lax.axis_size("tm"):
        steps.append(step)
        step *= 2
    return steps


def total(value, beside):
    value = value + core_swap(value)
    steps = [1] + far_strides()
    for step in steps[:-1]:
        value = stride_sum(value, step)
    return stride_sum(after(value, beside), steps[-1])


def local(coords, anomalies, noise_var):
    points = anomalies.shape[0]
    operands = [pltpu.with_memory_space_constraint(x, pltpu.HBM) for x in (coords, noise_var[None, :], anomalies)]
    given, whole, rows, ranks = sort_points(*operands)

    near = [pair_swap(c) for c in given]
    turned = pair_shift(given[-1], 1)
    mates = core_swap(whole)
    image, own_eval = eval_product(points, given[0], rows, (given,))
    near[0] = after(near[0], image[0], turned)
    far = [pair_shift(near[0])]
    image, mate_eval = eval_product(points, given[0], rows, ((after(mates, near[0]),),), image)
    near[1] = after(near[1], image[0])
    far.append(pair_shift(near[1]))
    far.append(pair_swap(after(turned, near[2], near[1])))
    near_mates = [core_swap(c) for c in near]
    image, near_eval = eval_product(points, given[0], rows, (near,), image)
    far = [after(c, image[0]) for c in far]
    far_mates = [core_swap(c) for c in far]
    image, far_eval = eval_product(points, given[0], rows, (far,), image)
    (*once, whole), rest_eval = eval_product(points, given[0], rows, (near_mates, far_mates), image, True)

    near = [pair_swap(c) for c in once]
    turned = pair_shift(once[-1], 1)
    mates = core_swap(whole)
    image0 = unsort(ranks, after(whole, mates))
    image = product(points, own_eval, rows, (once,))
    image = product(points, mate_eval, rows, ((after(mates, image0),),), image)
    near[0] = after(near[0], image[0], turned)
    far = [pair_shift(c) for c in near[:-1]]
    far.append(pair_swap(after(turned, near[-1], near[0])))
    near_mates = [core_swap(c) for c in near]
    image = product(points, near_eval, rows, (near,), image)
    far_mates = [core_swap(after(far[0], image[0])), core_swap(far[1]), core_swap(after(far[2], image[0]))]
    image = product(points, far_eval, rows, (far,), image)
    twice, sums = product(points, rest_eval, rows, (near_mates, far_mates), image, False, all_sums, given, once)
    image1 = unsort(ranks, twice)

    sums = total(sums, image1)
    rr0, curve0, once_once, given_twice, once_twice = [sums[k : k + 1] for k in range(5)]
    alpha0 = rr0 / curve0
    rr1 = rr0 - 2.0 * alpha0 * curve0 + alpha0 * alpha0 * once_once
    beta = rr1 / rr0
    more = 1.0 + beta
    curve1 = more * more * curve0 - more * alpha0 * (given_twice + once_once) + alpha0 * alpha0 * once_twice
    alpha1 = rr1 / curve1
    residual = anomalies - alpha0 * image0
    weights = alpha0 * anomalies + alpha1 * (residual + beta * anomalies)
    again = (image0 - alpha0 * image1) + beta * image0
    return weights, residual - alpha1 * again


def solution(mesh):
    placed = (
        P(None, ("region", "tm", "tile")),
        P(("region", "tm", "tile"), None),
        P(("region", "tm", "tile")),
    )
    return jax.shard_map(
        local,
        mesh=mesh,
        in_specs=placed,
        out_specs=(P(("region", "tm", "tile"), None), P(("region", "tm", "tile"), None)),
        check_vma=False,
    )
```

```python
import functools

import jax
import jax.numpy as jnp
from jax import lax
from jax.experimental import pallas as pl
from jax.experimental.pallas import tpu as pltpu
from jax.sharding import PartitionSpec as P

LANES = 128
ROWS = 224
SLOTS = 40
UNROLL = 8
EVAL_UNROLL = 4
FIRST_CUTS = (0, 6, 12, 16)
LATER_CUTS = (0, 6, 12, 16)
FAR = 1.0e6
F32 = jnp.float32
BF16 = jnp.bfloat16
MIB = 1 << 20


def vmem_spec():
    return pl.BlockSpec(memory_space=pltpu.VMEM)


def smem_spec():
    return pl.BlockSpec(memory_space=pltpu.SMEM)


def split2(value):
    high = value.astype(BF16)
    low = (value - high.astype(F32)).astype(BF16)
    return high, low


def list_length(points, halves):
    return halves * (points // LANES) * -(-points // ROWS) + UNROLL


def header_rows(points):
    return -(-(3 * (points // LANES) + 3) // 8) * 8


def piece_sizes(points, cuts):
    rows = [points // LANES * cut // 16 * LANES for cut in cuts]
    return [b - a for a, b in zip(rows, rows[1:])]


def spans(chunks, top):
    found, start = [], 0
    for c, chunk in enumerate(chunks):
        skip = top if c == 0 else 0
        found.append((chunk, start, skip, chunk.shape[0] - skip))
        start += chunk.shape[0] - skip
    return found


def group_rows(chunks, top, start):
    for chunk, begin, skip, size in spans(chunks, top):
        if begin <= start < begin + size:
            return chunk, slice(start - begin + skip, start - begin + skip + LANES)
    raise ValueError(start)


def read_rows(chunks, top, start):
    chunk, here = group_rows(chunks, top, start)
    return chunk[here, :]


def sort_kernel(points, coords_hbm, noise_hbm, values_hbm, *refs):
    pieces = len(FIRST_CUTS) - 1
    out_values, refs = refs[: pieces + 1], refs[pieces + 1 :]
    rows, ranks, coords, noise, values, xcol, facts, sorted_facts, sorted_values, rank_row, rank_smem, sems = refs
    fetches = [
        pltpu.make_async_copy(source, target, sems.at[k])
        for k, (source, target) in enumerate(((coords_hbm, coords), (noise_hbm, noise), (values_hbm, values)))
    ]
    for fetch in fetches:
        fetch.start()
    fetches[0].wait()
    groups = points // LANES
    for g in range(groups):
        here = slice(g * LANES, (g + 1) * LANES)
        xcol[here, :] = jnp.transpose(jnp.broadcast_to(coords[1:2, here], (LANES, LANES)))

    xrow = [jnp.broadcast_to(coords[1:2, g * LANES : (g + 1) * LANES], (8, LANES)) for g in range(groups)]
    lane = lax.broadcasted_iota(jnp.int32, (8, LANES), 1)
    sub = lax.broadcasted_iota(jnp.int32, (8, LANES), 0)
    counts = tuple(jnp.zeros((8, LANES), F32) for _ in range(groups))
    for jg in range(groups):

        def count(step, carry):
            at = pl.multiple_of(jg * LANES + step * 8, 8)
            mine = xcol[pl.ds(at, 8), :]
            out = []
            for ig in range(groups):
                if ig == jg:
                    before = jnp.logical_or(
                        mine < xrow[ig],
                        jnp.logical_and(mine == xrow[ig], sub + step * 8 < lane),
                    )
                elif ig > jg:
                    before = mine <= xrow[ig]
                else:
                    before = mine < xrow[ig]
                out.append(carry[ig] + jnp.where(before, 1.0, 0.0))
            return tuple(out)

        counts = lax.fori_loop(0, LANES // 8, count, counts, unroll=4)
    for g in range(groups):
        rank_row[0:1, g * LANES : (g + 1) * LANES] = jnp.sum(counts[g], axis=0, keepdims=True).astype(jnp.int32)
    ranks[...] = rank_row[...]
    copy = pltpu.make_async_copy(rank_row, rank_smem, sems.at[3])
    copy.start()
    fetches[1].wait()
    blank = jnp.zeros((LANES - 4, LANES), F32)
    for g in range(groups):
        here = slice(g * LANES, (g + 1) * LANES)
        facts[here, :] = jnp.transpose(jnp.concatenate([coords[:, here], noise[:, here], blank], axis=0))
    copy.wait()
    fetches[2].wait()

    def scatter(step, carry):
        at = pl.multiple_of(step * 8, 8)
        block = values[pl.ds(at, 8), :]
        fact = facts[pl.ds(at, 8), :]
        for k in range(8):
            to = rank_smem[0, at + k]
            sorted_facts[pl.ds(to, 1), :] = fact[k : k + 1, :]
            sorted_values[pl.ds(to, 1), :] = block[k : k + 1, :]
        return carry

    lax.fori_loop(0, points // 8, scatter, 0, unroll=8)
    header = header_rows(points)
    whole = out_values[pieces]
    whole[header:, :] = sorted_values[...]
    for chunk, start, skip, size in spans(out_values[:pieces], header):
        chunk[skip:, :] = sorted_values[start : start + size, :]
    head = out_values[0]
    for g in range(groups):
        here = slice(g * LANES, (g + 1) * LANES)
        got = sorted_facts[here, :]
        flat = jnp.transpose(got)
        for k in range(4):
            if k < 3:
                head[k * groups + g : k * groups + g + 1, :] = flat[k : k + 1, :]
            scale = 4.0 if k < 3 else 1.0
            rows[k, here, :] = jnp.broadcast_to(got[:, k : k + 1] * scale, (LANES, LANES))
    for k in range(4):
        rows[k, points:, :] = jnp.full((ROWS, LANES), FAR if k < 3 else 0.0, F32)
    end = 3 * groups
    head[end : end + 1, :] = jnp.full((1, LANES), jnp.min(coords[0:1, :]), F32)
    head[end + 1 : end + 2, :] = jnp.full((1, LANES), jnp.max(coords[0:1, :]), F32)
    head[end + 2 : header, :] = jnp.ones((header - end - 2, LANES), F32)
    whole[0:header, :] = head[0:header, :]


def sort_points(coords, noise, values):
    points, width = values.shape
    header = header_rows(points)
    sizes = piece_sizes(points, FIRST_CUTS)
    out = pl.pallas_call(
        functools.partial(sort_kernel, points),
        out_shape=tuple(
            jax.ShapeDtypeStruct((size + (header if c in (0, len(sizes)) else 0), width), F32)
            for c, size in enumerate([*sizes, points])
        )
        + (
            pltpu.VMEM((4, points + ROWS, LANES), F32),
            jax.ShapeDtypeStruct((1, points), jnp.int32),
        ),
        in_specs=[pl.BlockSpec(memory_space=pltpu.HBM)] * 3,
        out_specs=[vmem_spec()] * (len(sizes) + 3),
        scratch_shapes=[
            pltpu.VMEM((3, points), F32),
            pltpu.VMEM((1, points), F32),
            pltpu.VMEM((points, width), F32),
            pltpu.VMEM((points, LANES), F32),
            pltpu.VMEM((points, LANES), F32),
            pltpu.VMEM((points, LANES), F32),
            pltpu.VMEM((points, LANES), F32),
            pltpu.VMEM((1, points), jnp.int32),
            pltpu.SMEM((1, points), jnp.int32),
            pltpu.SemaphoreType.DMA((4,)),
        ],
        compiler_params=pltpu.CompilerParams(vmem_limit_bytes=14 * MIB),
        name="sort_points",
    )(coords, noise, values)
    return out[: len(sizes)], *out[len(sizes) :]


def tile_values(rows, cols, at, count):
    span = pl.ds(at, count)
    dtime = jnp.abs(rows[0, span, :] - cols[0])
    dx = rows[1, span, :] - cols[1]
    dy = rows[2, span, :] - cols[2]
    square = jnp.maximum(dx * dx + dy * dy, 1e-30)
    dist = square * lax.rsqrt(square)
    near = jnp.maximum(4.0 - dtime, 0.0) * jnp.maximum(4.0 - dist, 0.0)
    near = near * near
    return near * near * ((dtime + 1.0) * (dist + 1.0))


def fill_tile(tile, rows, facts, w, step, at):
    cols = [jnp.broadcast_to(facts[pl.ds(k * step + w, 1), :], (16, LANES)) for k in range(3)]
    for part in range(ROWS // 16):
        start = pl.multiple_of(at + part * 16, 16)
        high, low = split2(tile_values(rows, cols, start, 16))
        tile[part * 16 : (part + 1) * 16, 0:LANES] = high
        tile[part * 16 : (part + 1) * 16, LANES:] = low


def gather_facts(windows, facts, heads):
    for half, head in enumerate(heads):
        for k in range(3):
            base = (len(heads) * k + half) * windows
            facts[base : base + windows, :] = head[k * windows : (k + 1) * windows, :] * 4.0


def find_ranges(points, own, other):
    windows = points // LANES
    early, late, mark = 3 * windows, 3 * windows + 1, 3 * windows + 2
    x = other[windows : 2 * windows, :]
    low = jnp.broadcast_to(x[:, 0:1], (windows, LANES))
    high = jnp.broadcast_to(x[:, LANES - 1 : LANES], (windows, LANES))
    begin = jnp.zeros((windows, LANES), F32)
    beyond = jnp.zeros((windows, LANES), F32)
    for g in range(windows):
        row = jnp.broadcast_to(own[windows + g : windows + g + 1, :], (windows, LANES))
        begin = begin + jnp.where(low - row >= 1.0, 1.0, 0.0)
        beyond = beyond + jnp.where(row - high >= 1.0, 1.0, 0.0)
    begin = jnp.sum(begin, axis=1, keepdims=True)
    end = points - jnp.sum(beyond, axis=1, keepdims=True)
    first = begin.astype(jnp.int32) // 16 * 16
    length = end - first.astype(F32)
    blocks = jnp.zeros((windows, 1), F32)
    for k in range(-(-points // ROWS)):
        blocks = blocks + jnp.where(length > float(k * ROWS), 1.0, 0.0)
    apart = jnp.maximum(
        other[early : early + 1, 0:1] - own[late : late + 1, 0:1],
        own[early : early + 1, 0:1] - other[late : late + 1, 0:1],
    )
    apart = jnp.where(other[mark : mark + 1, 0:1] > 0.5, apart, 2.0)
    blocks = jnp.where(jnp.logical_and(end > begin, jnp.broadcast_to(apart, (windows, 1)) < 1.0), blocks, 0.0)
    return jnp.broadcast_to(first * 64 + blocks.astype(jnp.int32), (windows, LANES))


def list_tiles(points, own, heads, work, facts, table, table_smem, sem, beside):
    windows = points // LANES
    found = jnp.concatenate([find_ranges(points, own, head) for head in heads], axis=0)
    lane = lax.broadcasted_iota(jnp.int32, found.shape, 1)
    sub = lax.broadcasted_iota(jnp.int32, found.shape, 0)
    table[...] = jnp.sum(jnp.where(lane == sub, found, 0), axis=0, keepdims=True)
    copy = pltpu.make_async_copy(table, table_smem, sem)
    copy.start()
    gather_facts(windows, facts, heads)
    beside()
    copy.wait()
    slot = jnp.int32(0)
    for w in range(len(heads) * windows):
        packed = table_smem[0, w]
        first = lax.shift_right_logical(packed, 6)
        blocks = lax.bitwise_and(packed, 63)
        for b in range(2):
            work[0, slot + b] = first + b * ROWS
            work[1, slot + b] = w

        @pl.when(blocks > 2)
        def _(slot=slot, first=first, blocks=blocks, w=w):
            def block(b, carry):
                work[0, slot + b] = first + b * ROWS
                work[1, slot + b] = w
                return carry

            lax.fori_loop(2, blocks, block, 0)

        slot = slot + blocks
    for k in range(UNROLL):
        work[0, slot + k] = points
        work[1, slot + k] = 0
    work[2, 0] = slot
    return slot


def keep_tiles(windows, work, facts, rows, cache, step):
    for k in range(EVAL_UNROLL):
        s = step * EVAL_UNROLL + k
        fill_tile(cache.at[s], rows, facts, work[1, s], windows, pl.multiple_of(work[0, s], 16))


def kept_shapes(points, halves):
    return (
        pltpu.VMEM((SLOTS, ROWS, 2 * LANES), BF16),
        jax.ShapeDtypeStruct((3, list_length(points, halves)), jnp.int32),
        jax.ShapeDtypeStruct((3 * halves * (points // LANES), LANES), F32),
    )


def list_scratch():
    return [pltpu.VMEM((1, LANES), jnp.int32), pltpu.SMEM((1, LANES), jnp.int32), pltpu.SemaphoreType.DMA]


def light_cost():
    return pl.CostEstimate(flops=1_000_000, bytes_accessed=100_000, transcendentals=0)


def split_values(points, values, top, pairs):
    for half, chunks in enumerate(values):
        for chunk, start, skip, size in spans(chunks, top):
            base = half * (points // LANES) + start // LANES

            def split(w, carry):
                high, low = split2(chunk[pl.ds(pl.multiple_of(skip + w * LANES, 8), LANES), :])
                both = jnp.concatenate([high, low], axis=1)
                pairs[base + w, 0:LANES, :] = both
                pairs[base + w, LANES:, :] = both
                return carry

            lax.fori_loop(0, size // LANES, split, 0, unroll=2)


def multiply(work, cache, pairs, acc, step, count):
    for k in range(count):
        s = step * count + k
        at = pl.multiple_of(work[0, s], 16)
        acc[pl.ds(at, ROWS), :] += jnp.dot(cache[s], pairs[work[1, s]], preferred_element_type=F32)


def multiply_rest(windows, work, facts, rows, cache, pairs, acc, tile, total):
    slots = cache.shape[0]

    @pl.when(total > slots)
    def _():
        def again(s, carry):
            at = pl.multiple_of(work[0, s], 16)
            w = work[1, s]
            fill_tile(tile, rows, facts, w, windows, at)
            acc[pl.ds(at, ROWS), :] += jnp.dot(tile[...], pairs[w], preferred_element_type=F32)
            return carry

        lax.fori_loop(slots, total, again, 0)


def finish(points, header, top, marker, rows, acc, groups):
    first, (before, given, once, out, sums) = groups[0], groups[-5:]
    marks = [jnp.zeros((8, LANES), F32)] * 5
    for start in range(0, points, LANES):
        here = slice(start, start + LANES)
        image = (acc[here, 0:LANES] + acc[here, LANES:]) * (2.0**-16)
        if before:
            image = image + read_rows(before, 0, start)
        else:
            image = image + rows[3, here, :] * read_rows(first, top, start)
        if len(out) > 1:
            target, place = group_rows(out[:-1], 0, start)
            target[place, :] = image
        out[-1][here, :] = image
        if marker is not None:
            marks = marker(marks, image, read_rows(given, header, start), read_rows(once, 0, start))
    if marker is not None:
        sums[0][...] = jnp.zeros((8, LANES), F32)
        for k in range(5):
            sums[0][k : k + 1, :] = jnp.sum(marks[k], axis=0, keepdims=True)


def take_groups(refs, counts):
    groups = []
    for count in counts:
        groups.append(refs[:count])
        refs = refs[count:]
    return groups, refs


def product_kernel(points, halves, headed, counts, marker, work, facts, rows, cache, *refs):
    groups, (acc, pairs, tile) = take_groups(refs, counts)
    header = header_rows(points)
    top = header if headed else 0
    total = work[2, 0]
    acc[...] = jnp.zeros_like(acc)

    @pl.when(total > 0)
    def _():
        split_values(points, groups[:halves], top, pairs)

        def slots(step, carry):
            multiply(work, cache, pairs, acc, step, UNROLL)
            return carry

        kept = jnp.minimum(total, cache.shape[0])
        lax.fori_loop(0, (kept + (UNROLL - 1)) // UNROLL, slots, 0)
        multiply_rest(halves * (points // LANES), work, facts, rows, cache, pairs, acc, tile, total)

    finish(points, header, top, marker, rows, acc, groups)


def both_kernel(points, halves, counts, own, rows, *refs):
    windows = halves * (points // LANES)
    groups, refs = take_groups(refs, counts)
    values = groups[:halves]
    cache, work, facts, acc, pairs, tile, table, table_smem, sem = refs
    header = header_rows(points)

    def prepare():
        acc[...] = jnp.zeros_like(acc)
        split_values(points, values, header, pairs)

    heads = [half[0] for half in values]
    total = list_tiles(points, own, heads, work, facts, table, table_smem, sem, prepare)

    @pl.when(total > 0)
    def _():
        kept = jnp.minimum(total, cache.shape[0])
        steps = (kept + (EVAL_UNROLL - 1)) // EVAL_UNROLL
        keep_tiles(windows, work, facts, rows, cache, 0)

        def slots(step, carry):
            multiply(work, cache, pairs, acc, step - 1, EVAL_UNROLL)
            keep_tiles(windows, work, facts, rows, cache, step)
            return carry

        lax.fori_loop(1, steps, slots, 0)
        multiply(work, cache, pairs, acc, steps - 1, EVAL_UNROLL)
        multiply_rest(windows, work, facts, rows, cache, pairs, acc, tile, total)

    finish(points, header, header, None, rows, acc, groups)


def product_scratch(points, halves):
    return [
        pltpu.VMEM((points + ROWS, 2 * LANES), F32),
        pltpu.VMEM((halves * (points // LANES), 2 * LANES, 2 * LANES), BF16),
        pltpu.VMEM((ROWS, 2 * LANES), BF16),
    ]


def image_shapes(points, sent):
    sizes = [*(piece_sizes(points, LATER_CUTS) if sent else []), points]
    return [jax.ShapeDtypeStruct((size, LANES), F32) for size in sizes]


def fold(value):
    return jnp.sum(value.reshape(value.shape[0] // 8, 8, LANES), axis=0)


def all_sums(marks, image, given, once):
    terms = (given * given, given * once, once * once, given * image, once * image)
    return [mark + fold(term) for mark, term in zip(marks, terms)]


def product(points, evaluated, rows, values, before=(), headed=False, marker=None, given=(), once=()):
    cache, work, facts = evaluated
    groups = (*values, before, given, once)
    operands = (facts, rows, cache, *(x for group in groups for x in group))
    sums = int(marker is not None)
    counts = [len(group) for group in groups] + [1, sums]
    out = pl.pallas_call(
        functools.partial(product_kernel, points, len(values), headed, counts, marker),
        out_shape=image_shapes(points, False) + [jax.ShapeDtypeStruct((8, LANES), F32)] * sums,
        in_specs=[smem_spec()] + [vmem_spec()] * len(operands),
        out_specs=[vmem_spec()] * (1 + sums),
        scratch_shapes=product_scratch(points, len(values)),
        compiler_params=pltpu.CompilerParams(vmem_limit_bytes=15 * MIB),
        cost_estimate=light_cost(),
        name="product",
    )(work, *operands)
    return tuple(out)


def eval_product(points, own, rows, values, before=(), sent=False):
    halves = len(values)
    groups = (*values, before, (), ())
    operands = (own, rows, *(x for group in groups for x in group))
    images = image_shapes(points, sent)
    counts = [len(group) for group in groups] + [len(images), 0]
    out = pl.pallas_call(
        functools.partial(both_kernel, points, halves, counts),
        out_shape=(*images, *kept_shapes(points, halves)),
        in_specs=[vmem_spec()] * len(operands),
        out_specs=(*[vmem_spec()] * (len(images) + 1), smem_spec(), vmem_spec()),
        scratch_shapes=product_scratch(points, halves) + list_scratch(),
        compiler_params=pltpu.CompilerParams(vmem_limit_bytes=15 * MIB),
        cost_estimate=light_cost(),
        name="eval_product",
    )(*operands)
    return tuple(out[: len(images)]), tuple(out[len(images) :])


def unsort_kernel(points, ranks, source, out):
    def gather(step, carry):
        at = pl.multiple_of(step * 8, 8)
        out[pl.ds(at, 8), :] = jnp.concatenate(
            [source[pl.ds(ranks[0, at + k], 1), :] for k in range(8)], axis=0
        )
        return carry

    lax.fori_loop(0, points // 8, gather, 0, unroll=8)


def unsort(ranks, source):
    points = ranks.shape[1]
    return pl.pallas_call(
        functools.partial(unsort_kernel, points),
        out_shape=jax.ShapeDtypeStruct((points, LANES), F32),
        in_specs=[smem_spec(), vmem_spec()],
        out_specs=vmem_spec(),
        compiler_params=pltpu.CompilerParams(vmem_limit_bytes=8 * MIB),
        cost_estimate=light_cost(),
        name="unsort",
    )(ranks, source)


def pair_swap(block):
    count = lax.axis_size("tm")
    return lax.ppermute(block, "tm", [(i, i ^ 1) for i in range(count)])


def pair_shift(block, turn=0):
    count = lax.axis_size("tm")
    route = []
    for i in range(count):
        source = i - 2 if i % 2 == turn else i + 2
        if 0 <= source < count:
            route.append((source, i))
    return lax.ppermute(block, "tm", route)


def core_swap(block):
    count = lax.axis_size("tile")
    return lax.ppermute(block, "tile", [(i, i ^ 1) for i in range(count)])


def after(value, *earlier):
    return lax.optimization_barrier((value, *earlier))[0]


def stride_sum(value, step):
    count = lax.axis_size("tm")
    return value + lax.ppermute(value, "tm", [(i, i ^ step) for i in range(count)])


def far_strides():
    step, steps = 2, []
    while step < lax.axis_size("tm"):
        steps.append(step)
        step *= 2
    return steps


def total(value, beside):
    value = value + core_swap(value)
    steps = [1] + far_strides()
    for step in steps[:-1]:
        value = stride_sum(value, step)
    return stride_sum(after(value, beside), steps[-1])


def local(coords, anomalies, noise_var):
    points = anomalies.shape[0]
    operands = [pltpu.with_memory_space_constraint(x, pltpu.HBM) for x in (coords, noise_var[None, :], anomalies)]
    given, whole, rows, ranks = sort_points(*operands)

    near = [pair_swap(c) for c in given]
    turned = pair_shift(given[-1], 1)
    mates = core_swap(whole)
    image, own_eval = eval_product(points, given[0], rows, (given,))
    near[0] = after(near[0], image[0], turned)
    far = [pair_shift(near[0])]
    image, mate_eval = eval_product(points, given[0], rows, ((after(mates, near[0]),),), image)
    near[1] = after(near[1], image[0])
    far.append(pair_shift(near[1]))
    far.append(pair_swap(after(turned, near[2], near[1])))
    near_mates = [core_swap(c) for c in near]
    image, near_eval = eval_product(points, given[0], rows, (near,), image)
    far_mates = [core_swap(far[0]), *(core_swap(after(c, image[0])) for c in far[1:])]
    image, far_eval = eval_product(points, given[0], rows, (far,), image)
    (*once, whole), rest_eval = eval_product(points, given[0], rows, (near_mates, far_mates), image, True)

    near = [pair_swap(c) for c in once]
    turned = pair_shift(once[-1], 1)
    mates = core_swap(whole)
    image0 = unsort(ranks, after(whole, mates))
    image = product(points, own_eval, rows, (once,))
    image = product(points, mate_eval, rows, ((after(mates, image0),),), image)
    near[0] = after(near[0], image[0], turned)
    far = [pair_shift(c) for c in near[:-1]]
    far.append(pair_swap(after(turned, near[-1], near[0])))
    near_mates = [core_swap(c) for c in near]
    image = product(points, near_eval, rows, (near,), image)
    far_mates = [core_swap(after(far[0], image[0])), core_swap(far[1]), core_swap(after(far[2], image[0]))]
    image = product(points, far_eval, rows, (far,), image)
    twice, sums = product(points, rest_eval, rows, (near_mates, far_mates), image, False, all_sums, given, once)
    image1 = unsort(ranks, twice)

    sums = total(sums, image1)
    rr0, curve0, once_once, given_twice, once_twice = [sums[k : k + 1] for k in range(5)]
    alpha0 = rr0 / curve0
    rr1 = rr0 - 2.0 * alpha0 * curve0 + alpha0 * alpha0 * once_once
    beta = rr1 / rr0
    more = 1.0 + beta
    curve1 = more * more * curve0 - more * alpha0 * (given_twice + once_once) + alpha0 * alpha0 * once_twice
    alpha1 = rr1 / curve1
    residual = anomalies - alpha0 * image0
    weights = alpha0 * anomalies + alpha1 * (residual + beta * anomalies)
    again = (image0 - alpha0 * image1) + beta * image0
    return weights, residual - alpha1 * again


def solution(mesh):
    placed = (
        P(None, ("region", "tm", "tile")),
        P(("region", "tm", "tile"), None),
        P(("region", "tm", "tile")),
    )
    return jax.shard_map(
        local,
        mesh=mesh,
        in_specs=placed,
        out_specs=(P(("region", "tm", "tile"), None), P(("region", "tm", "tile"), None)),
        check_vma=False,
    )
```
